32 devices in a mesh: row: 4 (over y, core), col: 8 (over z, x).
Axes of the slice: x: 2, y: 2, z: 4, core: 2. Of those that a mesh axis runs over, the one named last changes fastest.
Arguments:
- inputs: bfloat16 [1024, 8192], P('col', 'row'), may hold values from -6 to 6
- grad_out: bfloat16 [1024, 8192], P('col', 'row'), may hold values from -0.59765625 to 0.59765625
- gate_pre: bfloat16 [1024, 14336], P('row', 'col'), may hold values from -9 to 9
- up_pre: bfloat16 [1024, 14336], P('row', 'col'), may hold values from -6 to 6
- w_gate: bfloat16 [8192, 14336], P('row', 'col'), may hold values from -0.125 to 0.125
- w_up: bfloat16 [8192, 14336], P('row', 'col'), may hold values from -0.125 to 0.125
- w_down: bfloat16 [14336, 8192], P('col', 'row'), may hold values from -0.09375 to 0.09375
- mask_gate: int32 [64, 112], P('row', 'col'), may hold values 0 or 1
- mask_up: int32 [64, 112], P('row', 'col'), may hold values 0 or 1
- mask_down: int32 [112, 64], P('col', 'row'), may hold values 0 or 1
Outputs:
- grad_inputs: bfloat16 [1024, 8192], P('col', 'row')
- grad_gate: bfloat16 [8192, 14336], P('row', 'col')
- grad_up: bfloat16 [8192, 14336], P('row', 'col')
- grad_down: bfloat16 [14336, 8192], P('col', 'row')
The draws below stay inside these ranges and needn't reach their ends.
All inputs are finite; a program needn't handle non-finite values. No bound on the sum of `mask_gate` or of `mask_up` or of `mask_down` on one device may be relied on, other than what follows from the above.
Results may differ from the reference program's by a relative error of at most 0.005.
Values may be sent and summed in bfloat16 or wider, within the bound.
No kernel may reach another device: no remote copies, remote signals or barrier semaphores. Data moves between devices by JAX's collectives and lax.ppermute only.
A program may use at most 128 MiB of HBM per device.

```python
import jax
import jax.numpy as jnp
from jax import lax

D = 8192
FF = 14336
BLK = 128
TOKENS = 1024


def with_ends(values, key, least, top_value):
    shape = values.shape
    index_at = [jax.random.randint(jax.random.fold_in(key, axis), (), 0, shape[axis]) for axis in range(len(shape))]
    values = values.at[tuple(index_at)].set(least)
    longest = shape.index(max(shape))
    index_at[longest] = (index_at[longest] + 1) % shape[longest]
    return values.at[tuple(index_at)].set(top_value)


def block_levels(stream_key, dims, split, smallest, high):
    factor_of = 1.0
    for axis_at, blocks in split:
        heights = jax.random.uniform(jax.random.fold_in(jax.random.fold_in(stream_key, 6), axis_at), (blocks,), jnp.float32, smallest / len(split), high / len(split))
        factor_of = factor_of * jnp.repeat(jnp.exp(heights), dims[axis_at] // blocks).reshape((-1,) + (1,) * (len(dims) - 1 - axis_at))
    return factor_of


def gaussian(own_key, dims, width, limit, shards=(), kind=jnp.bfloat16):
    level = block_levels(own_key, dims, shards, -0.22, 0.18) if shards else 1.0
    array = jax.random.normal(own_key, dims, jnp.float32) * width * level
    return jnp.minimum(jnp.maximum(array, -limit), limit).astype(kind)


def setup_inputs(seed: int = 0) -> dict:
    splits = jax.random.split(jax.random.key(seed), 11)
    return {
        "inputs": gaussian(splits[0], (TOKENS, D), 1.0, 6.0, ((0, 8), (1, 4))),
        "grad_out": gaussian(splits[1], (TOKENS, D), 0.1, 0.59765625, ((0, 8), (1, 4))),
        "gate_pre": gaussian(splits[2], (TOKENS, FF), 1.5, 9.0, ((0, 4), (1, 8))),
        "up_pre": gaussian(splits[3], (TOKENS, FF), 1.0, 6.0, ((0, 4), (1, 8))),
        "w_gate": gaussian(splits[4], (D, FF), (3 * D // 10) ** -0.5, 0.125, ((0, 4), (1, 8))),
        "w_up": gaussian(splits[5], (D, FF), (3 * D // 10) ** -0.5, 0.125, ((0, 4), (1, 8))),
        "w_down": gaussian(splits[6], (FF, D), (3 * FF // 10) ** -0.5, 0.09375, ((0, 8), (1, 4))),
        "mask_gate": with_ends((jax.random.randint(splits[7], (D // BLK, FF // BLK), 0, 10) < 3).astype(jnp.int32), jax.random.fold_in(splits[7], 1), 0, 1),
        "mask_up": with_ends((jax.random.randint(splits[8], (D // BLK, FF // BLK), 0, 10) < 3).astype(jnp.int32), jax.random.fold_in(splits[8], 1), 0, 1),
        "mask_down": with_ends((jax.random.randint(splits[9], (FF // BLK, D // BLK), 0, 10) < 3).astype(jnp.int32), jax.random.fold_in(splits[9], 1), 0, 1),
    }


def expand(mask):
    return jnp.repeat(jnp.repeat(mask, BLK, 0), BLK, 1).astype(jnp.bfloat16)


def reference(inputs, grad_out, gate_pre, up_pre, w_gate, w_up, w_down, mask_gate, mask_up, mask_down):
    keep_gate = expand(mask_gate)
    keep_up = expand(mask_up)
    keep_down = expand(mask_down)
    gate_eff = w_gate * keep_gate
    up_eff = w_up * keep_up
    down_eff = w_down * keep_down
    hidden_grad = lax.dot_general(grad_out, down_eff, (((1,), (1,)), ((), ())), preferred_element_type=jnp.float32)
    gated = gate_pre.astype(jnp.float32)
    upper = up_pre.astype(jnp.float32)
    sigma = jax.nn.sigmoid(gated)
    act = (gated * sigma * upper).astype(jnp.bfloat16)
    grad_g = (hidden_grad * upper * sigma * (1.0 + gated * (1.0 - sigma))).astype(jnp.bfloat16)
    grad_u = (hidden_grad * gated * sigma).astype(jnp.bfloat16)
    contract = (((1,), (1,)), ((), ()))
    grad_inputs = lax.dot_general(grad_g, gate_eff, contract, preferred_element_type=jnp.float32)
    grad_inputs = grad_inputs + lax.dot_general(grad_u, up_eff, contract, preferred_element_type=jnp.float32)
    tokens_dim = (((0,), (0,)), ((), ()))
    grad_gate = lax.dot_general(inputs, grad_g, tokens_dim, preferred_element_type=jnp.float32) * keep_gate.astype(jnp.float32)
    grad_up = lax.dot_general(inputs, grad_u, tokens_dim, preferred_element_type=jnp.float32) * keep_up.astype(jnp.float32)
    grad_down = lax.dot_general(act, grad_out, tokens_dim, preferred_element_type=jnp.float32) * keep_down.astype(jnp.float32)
    return (grad_inputs.astype(jnp.bfloat16), grad_gate.astype(jnp.bfloat16), grad_up.astype(jnp.bfloat16), grad_down.astype(jnp.bfloat16))
```

```python
import functools

import jax
import jax.numpy as jnp
from jax import lax
from jax.experimental import pallas as pl
from jax.experimental.pallas import tpu as pltpu
from jax.sharding import PartitionSpec as P

F32 = jnp.float32
BF16 = jnp.bfloat16
MIB = 1024 * 1024
NT = (((1,), (1,)), ((), ()))
NN = (((1,), (0,)), ((), ()))


def params(mib):
    return pltpu.CompilerParams(vmem_limit_bytes=mib * MIB)


def cost(flops, nbytes):
    return pl.CostEstimate(flops=flops // 4096, bytes_accessed=nbytes // 4096, transcendentals=0)


def smem_spec():
    return pl.BlockSpec(memory_space=pltpu.SMEM)


def whole_spec(x):
    return pl.BlockSpec(x.shape, lambda *_: (0,) * x.ndim, pipeline_mode=pl.Buffered(1))


def in_hbm(x):
    return pltpu.with_memory_space_constraint(x, pltpu.HBM)


def stack_rows(dst_ref, refs):
    at = 0
    for r in refs:
        dst_ref[at : at + r.shape[0]] = r[...]
        at += r.shape[0]


def tile_copy(w_ref, dst_ref, sem_ref, t):
    rows = dst_ref.shape[1]
    at = pl.ds(pl.multiple_of(t * rows, rows), rows)
    return pltpu.make_async_copy(w_ref.at[at], dst_ref.at[t], sem_ref.at[t])


def apply_mask(dst_ref, w_ref, m_ref, i, blk):
    for a in range(2):
        for j in range(w_ref.shape[1] // blk):
            keep = m_ref[2 * i + a, j].astype(F32).astype(BF16)
            ra, cj = slice(a * blk, (a + 1) * blk), slice(j * blk, (j + 1) * blk)
            dst_ref[ra, cj] = w_ref[ra, cj] * keep


def hidden_part(where, first, second, w, mask, swap):
    h, d = w.shape
    blk = h // mask.shape[0]
    m = first.shape[0]
    tile = 2 * blk

    def body(at_ref, m_ref, w_ref, a_ref, b_ref, keep_ref, send_ref, rows_ref, eff_ref, all_ref, sem_ref, row_sem):
        j = pl.program_id(0)

        @pl.when(j == 0)
        def _():
            rows = [
                pltpu.make_async_copy(x, rows_ref.at[pl.ds(i * m, m)], row_sem.at[i])
                for i, x in enumerate((a_ref, b_ref))
            ]
            for copy in rows:
                copy.start()
            for t in range(h // tile):
                tile_copy(w_ref, all_ref, sem_ref, t).start()
            for copy in rows:
                copy.wait()

        tile_copy(w_ref, all_ref, sem_ref, j).wait()
        apply_mask(eff_ref, all_ref.at[j], m_ref, j, blk)
        out = lax.dot_general(rows_ref[...], eff_ref[...], NT, preferred_element_type=F32)
        one, two = out[:m], out[m:]
        if swap:
            here = at_ref[where.shape[0] - 1] == 0
            one, two = jnp.where(here, one, two), jnp.where(here, two, one)
        keep_ref[...] = one
        send_ref[...] = two.astype(BF16)

    out_spec = pl.BlockSpec((m, tile), lambda j: (0, j))
    return pl.pallas_call(
        body,
        grid=(h // tile,),
        in_specs=[
            smem_spec(),
            smem_spec(),
        ]
        + [pl.BlockSpec(memory_space=pl.ANY)] * 3,
        out_specs=[out_spec, out_spec],
        out_shape=[jax.ShapeDtypeStruct((m, h), F32), jax.ShapeDtypeStruct((m, h), BF16)],
        scratch_shapes=[
            pltpu.VMEM((2 * m, d), BF16),
            pltpu.VMEM((tile, d), BF16),
            pltpu.VMEM((h // tile, tile, d), BF16),
            pltpu.SemaphoreType.DMA((h // tile,)),
            pltpu.SemaphoreType.DMA((2,)),
        ],
        compiler_params=params(16),
        cost_estimate=cost(4 * m * d * h, 2 * d * (m + h) + 6 * m * h),
        name="hidden_part",
    )(where, mask, in_hbm(w), first, second)


def activation(saved, where):
    m, h = saved[0][0].shape
    n = len(saved)
    wide = 256 if h % 256 == 0 else 128

    def body(at_ref, *refs):
        o_ref, buf_ref, sem_ref = refs[2 * n :]
        k = pl.program_id(0)

        def copy(src, i, p):
            return pltpu.make_async_copy(refs[2 * src + p], buf_ref.at[i, p], sem_ref.at[i, p])

        @pl.when(k == 0)
        def _():
            for i in range(n):
                for p in range(2):
                    copy(i, i, p).start()

        for p in range(2):
            copy(0, k, p).wait()
        for c in range(h // wide):
            at = slice(c * wide, (c + 1) * wide)
            g = buf_ref[k, 0, :, at].astype(F32)
            u = buf_ref[k, 1, :, at].astype(F32)
            act = g * (1.0 / (1.0 + jnp.exp(-g))) * u
            o_ref[at, :] = act.astype(BF16).T

    return pl.pallas_call(
        body,
        grid=(n,),
        in_specs=[smem_spec()] + [pl.BlockSpec(memory_space=pl.ANY)] * (2 * n),
        out_specs=pl.BlockSpec((h, m), lambda k: (0, k)),
        out_shape=jax.ShapeDtypeStruct((h, n * m), BF16),
        scratch_shapes=[pltpu.VMEM((n, 2, m, h), BF16), pltpu.SemaphoreType.DMA((n, 2))],
        compiler_params=params(16),
        cost_estimate=cost(10 * h * n * m, 6 * h * n * m),
        name="activation",
    )(where, *[in_hbm(x) for pair in saved for x in pair])


def swiglu_grads(sums, saved, where, n, q):
    m, h = sums[0].shape
    cuts = 2 if (h // 2) % 128 == 0 else 1
    wide = h // cuts
    ns, nt = len(saved), len(sums)

    def body(i_ref, *refs):
        s_refs, t_refs = refs[: 2 * ns], refs[2 * ns : 2 * ns + nt]
        o_ref, s_buf = refs[2 * ns + nt], refs[2 * ns + nt + 1]
        t_bufs = refs[2 * ns + nt + 2 : 2 * ns + 2 * nt + 2]
        o_buf, s_sem, t_sem, o_sem = refs[2 * ns + 2 * nt + 2 :]
        src = i_ref[n] // q
        rows = pl.ds(pl.multiple_of(i_ref[n] % q * m, m), m)

        def saved_copy(c, k, p):
            cols = slice(c * wide, (c + 1) * wide)
            return pltpu.make_async_copy(
                s_refs[2 * k + p].at[rows, cols], s_buf.at[c, p], s_sem.at[c, p]
            )

        def term_copy(c, t):
            cols = slice(c * wide, (c + 1) * wide)
            return pltpu.make_async_copy(t_refs[t].at[:, cols], t_bufs[t].at[c], t_sem.at[c, t])

        def out_copy(c):
            cols = slice(c * wide, (c + 1) * wide)
            return pltpu.make_async_copy(o_buf.at[c], o_ref.at[:, :, cols], o_sem.at[c])

        for c in range(cuts):
            for k in range(ns):

                @pl.when(src == k)
                def _():
                    for p in range(2):
                        saved_copy(c, k, p).start()

            for t in range(nt):
                term_copy(c, t).start()
        for c in range(cuts):
            for p in range(2):
                saved_copy(c, 0, p).wait()
            for t in range(nt):
                term_copy(c, t).wait()
            hg = t_bufs[0][c].astype(F32)
            for t in range(1, nt):
                hg = hg + t_bufs[t][c].astype(F32)
            g = s_buf[c, 0].astype(F32)
            u = s_buf[c, 1].astype(F32)
            sig = 1.0 / (1.0 + jnp.exp(-g))
            hs = hg * sig
            o_buf[c, 0] = (hs * u * (1.0 + g * (1.0 - sig))).astype(BF16)
            o_buf[c, 1] = (hs * g).astype(BF16)
            out_copy(c).start()
        for c in range(cuts):
            out_copy(c).wait()

    anywhere = pl.BlockSpec(memory_space=pl.ANY)
    return pl.pallas_call(
        body,
        in_specs=[smem_spec()] + [anywhere] * (2 * ns + nt),
        out_specs=anywhere,
        out_shape=jax.ShapeDtypeStruct((2, m, h), BF16),
        scratch_shapes=[pltpu.VMEM((cuts, 2, m, wide), BF16)]
        + [pltpu.VMEM((cuts, m, wide), x.dtype) for x in sums]
        + [
            pltpu.VMEM((cuts, 2, m, wide), BF16),
            pltpu.SemaphoreType.DMA((cuts, 2)),
            pltpu.SemaphoreType.DMA((cuts, nt)),
            pltpu.SemaphoreType.DMA((cuts,)),
        ],
        compiler_params=params(8),
        cost_estimate=cost(20 * h * m, 14 * h * m),
        name="swiglu_grads",
    )(where, *[in_hbm(x) for pair in saved for x in pair], *sums)


def turned_weight(w, mask, where):
    d, h = w.shape
    nr, nc = mask.shape
    blk = d // nr
    tile = 2 * blk

    def body(at_ref, m_ref, w_ref, o_ref):
        i = pl.program_id(0)
        for j in range(nc):
            cols = slice(j * blk, (j + 1) * blk)
            halves = []
            for a in range(2):
                keep = m_ref[2 * i + a, j].astype(F32).astype(BF16)
                halves.append(w_ref[a * blk : (a + 1) * blk, cols] * keep)
            o_ref[0, cols, :] = jnp.concatenate(halves, 0).T

    return pl.pallas_call(
        body,
        grid=(d // tile,),
        in_specs=[smem_spec(), smem_spec(), pl.BlockSpec((tile, h), lambda i: (i, 0))],
        out_specs=pl.BlockSpec((1, h, tile), lambda i: (i, 0, 0)),
        out_shape=pltpu.HBM((d // tile, h, tile), BF16),
        compiler_params=params(8),
        cost_estimate=cost(d * h, 4 * d * h),
        name="turned_weight",
    )(where, mask, in_hbm(w))


def input_part(grads, gate_t, up_t, where):
    _, m, h = grads[0].shape
    n = len(grads)
    tiles, _, tile = gate_t.shape
    d = tiles * tile

    def body(at_ref, wg_ref, wu_ref, *refs):
        o_ref, g_ref, u_ref, wg_all, wu_all, g_sem, u_sem, row_sem = refs[n:]
        i = pl.program_id(0)

        def copies(t):
            return (
                pltpu.make_async_copy(wg_ref.at[t], wg_all.at[t], g_sem.at[t]),
                pltpu.make_async_copy(wu_ref.at[t], wu_all.at[t], u_sem.at[t]),
            )

        @pl.when(i == 0)
        def _():
            rows = [
                pltpu.make_async_copy(r.at[p], dst.at[pl.ds(k * m, m)], row_sem.at[p, k])
                for p, dst in enumerate((g_ref, u_ref))
                for k, r in enumerate(refs[:n])
            ]
            for copy in rows:
                copy.start()
            for t in range(tiles):
                for copy in copies(t):
                    copy.start()
            for copy in rows:
                copy.wait()

        for copy in copies(i):
            copy.wait()
        out = lax.dot_general(g_ref[...], wg_all[i], NN, preferred_element_type=F32)
        out = out + lax.dot_general(u_ref[...], wu_all[i], NN, preferred_element_type=F32)
        for k in range(n):
            o_ref[k] = out[k * m : (k + 1) * m]

    anywhere = pl.BlockSpec(memory_space=pl.ANY)
    return pl.pallas_call(
        body,
        grid=(tiles,),
        in_specs=[smem_spec()] + [anywhere] * (2 + n),
        out_specs=pl.BlockSpec((n, m, tile), lambda j: (0, 0, j)),
        out_shape=jax.ShapeDtypeStruct((n, m, d), F32),
        scratch_shapes=[pltpu.VMEM((n * m, h), BF16)] * 2
        + [pltpu.VMEM((tiles, h, tile), BF16)] * 2
        + [pltpu.SemaphoreType.DMA((tiles,))] * 2
        + [pltpu.SemaphoreType.DMA((2, n))],
        compiler_params=params(28),
        cost_estimate=cost(4 * n * m * d * h, 4 * n * m * h + 4 * d * h + 4 * n * m * d),
        name="input_part",
    )(where, in_hbm(gate_t), in_hbm(up_t), *grads)


def weight_grad(lhs, rhs, mask, where, pick=None, places=None):
    lhs = lhs if isinstance(lhs, list) else [lhs]
    rows = lhs[0].shape[0]
    k = sum(x.shape[1] for x in lhs)
    cols = rhs[0].shape[-1]
    nr, nc = mask.shape
    blk = rows // nr
    per = 4 if nr % 4 == 0 else 2
    tile = per * blk
    wide = 2 * blk
    nl, n = len(lhs), len(rhs)

    def body(m_ref, p_ref, *refs):
        lefts, rights = refs[:nl], refs[nl : nl + n]
        o_ref, r_ref, l_ref = refs[nl + n :]
        i = pl.program_id(0)

        @pl.when(i == 0)
        def _():
            if places is None:
                stack_rows(r_ref, [r if pick is None else r.at[0] for r in rights])
            else:
                for t, r in enumerate(rights):
                    m = r.shape[0]
                    r_ref[pl.ds(pl.multiple_of(p_ref[places + t] * m, m), m)] = r[...]

        if nl > 1:
            at = 0
            for r in lefts:
                l_ref[:, at : at + r.shape[1]] = r[...]
                at += r.shape[1]
        left = l_ref if nl > 1 else lefts[0]
        for c in range(cols // wide):
            out = lax.dot_general(
                left[...], r_ref[:, c * wide : (c + 1) * wide], NN, preferred_element_type=F32
            )
            for a in range(per):
                for s in range(2):
                    keep = m_ref[i * per + a, 2 * c + s].astype(F32)
                    ra, cs = slice(a * blk, (a + 1) * blk), slice(s * blk, (s + 1) * blk)
                    at = slice((2 * c + s) * blk, (2 * c + s + 1) * blk)
                    o_ref[ra, at] = (out[ra, cs] * keep).astype(BF16)

    specs = [pl.BlockSpec((tile, x.shape[1]), lambda i: (i, 0)) for x in lhs]
    for r in rhs:
        if pick is None:
            specs.append(whole_spec(r))
        else:
            specs.append(
                pl.BlockSpec(
                    (1,) + r.shape[1:], lambda i: (pick, 0, 0), pipeline_mode=pl.Buffered(1)
                )
            )
    return pl.pallas_call(
        body,
        grid=(rows // tile,),
        in_specs=[smem_spec(), smem_spec()] + specs,
        out_specs=pl.BlockSpec((tile, cols), lambda i: (i, 0)),
        out_shape=jax.ShapeDtypeStruct((rows, cols), BF16),
        scratch_shapes=[
            pltpu.VMEM((k, cols), BF16),
            pltpu.VMEM((tile, k) if nl > 1 else (16, 128), BF16),
        ],
        compiler_params=params(20),
        cost_estimate=cost(2 * rows * cols * k, 2 * (rows * k + cols * k + rows * cols)),
        name="weight_grad",
    )(mask, where, *lhs, *rhs)


def join(*xs):
    return lax.optimization_barrier(xs)


def ring_order(n):
    a = 4 if n % 4 == 0 and n > 4 else 2
    b = n // a
    walk = [(0, j) for j in range(b)]
    for i in range(1, a):
        js = range(b - 1, 0, -1) if i % 2 else range(1, b)
        walk += [(i, j) for j in js]
    walk += [(i, 0) for i in range(a - 1, 0, -1)]
    return [i * b + j for i, j in walk]


def per_device(
    n_row, n_col, inputs, grad_out, gate_pre, up_pre, w_gate, w_up, w_down, mask_gate, mask_up, mask_down
):
    order = ring_order(n_col)
    half = n_col // 2
    ny = n_row // 2
    tpc = inputs.shape[0]
    q = gate_pre.shape[0] // tpc
    row = lax.axis_index("row")
    core = row % 2
    first = core == 0

    def ring_perm(step):
        pairs = []
        for r in range(n_row):
            s = step if r % 2 == 0 else -step
            for p in range(n_col):
                pairs.append((r * n_col + order[p], r * n_col + order[(p + s) % n_col]))
        return pairs

    back, ahead = ring_perm(-1), ring_perm(1)

    def from_ahead(x):
        return lax.ppermute(x, ("row", "col"), back)

    def from_behind(x):
        return lax.ppermute(x, ("row", "col"), ahead)

    def swap_core(x):
        return lax.ppermute(x, "row", [(r, r ^ 1) for r in range(n_row)])

    def shift_y(x, s):
        return lax.ppermute(
            x, "row", [(r, (r // 2 + s) % ny * 2 + r % 2) for r in range(n_row)]
        )

    last = half - 1
    dists = list(range(1, half)) + [0] + [s * d for d in range(1, half) for s in (1, -1)] + [0, half]
    at = lax.iota(jnp.int32, len(dists) + 1)
    dist = jnp.zeros_like(at)
    for i, d in enumerate(dists):
        if d:
            dist = jnp.where(at == i, d, dist)
    dist = jnp.where(at == last, core * half, dist)
    col = lax.axis_index("col")
    pos = sum(jnp.where(col == c, p, 0) for p, c in enumerate(order))
    near = (pos + (1 - 2 * core) * dist + 2 * n_col) % n_col
    block = sum(jnp.where(near == p, c, 0) for p, c in enumerate(order))
    owner = block // q
    s = (row // 2 - owner // 2 + ny) % ny
    e = (owner % 2 + core) % 2
    where = jnp.where(at == len(dists), core, (s * 2 + e) * q + block % q).astype(jnp.int32)

    def spread_y(x):
        return [shift_y(x, s) for s in range(1, ny)]

    go_rows, terms = [], []
    others, own, got, parts = [None] * half, [None] * half, [None] * half, [None] * half

    def hidden(n, x, y, after):
        kept, sent = hidden_part(after, x, y, w_down, mask_down, n == last)
        go_rows.extend([x, y])
        terms.append([kept, swap_core(sent)])

    def chip_sum(n):
        chip = (terms[n][0] + terms[n][1].astype(F32)).astype(BF16)
        return jnp.pad(chip, ((0, 0), (0, 128)))

    def grads(n, after):
        sums = terms[n] + others[n]
        if n == half - 2:
            sums = [in_hbm(x) for x in sums]
        own[n] = swiglu_grads(sums, saved, after, n, q)

    def following(x):
        return join(where, x)[0]

    a, b = from_ahead(grad_out), from_behind(grad_out)
    gate_y, up_y, in_t = spread_y(gate_pre), spread_y(up_pre), inputs.T
    by_core = []
    gate_t = turned_weight(w_gate, mask_gate, where)
    a, b, where, in_t, gate_t, *by_core = join(a, b, where, in_t, gate_t, *by_core)

    up_t, y_core = None, []
    for k in range(2, half + 1):
        na = from_ahead(a)
        nb = from_behind(b) if k < half else b
        after = where
        if k > 2:
            chip = chip_sum(k - 3)
            after = following(chip)
        hidden(k - 2, a, b, after)
        over, more = [], []
        if k > 2:
            over = others[k - 3] = spread_y(chip)
        if k == 2:
            up_t = turned_weight(w_up, mask_up, following(terms[0][0]))
            more = gate_y + up_y + [up_t]
        elif k == 3:
            by_core = [swap_core(gate_pre)]
            more = by_core
        elif k == 4:
            by_core = by_core + [swap_core(up_pre)]
            y_core = [swap_core(x) for x in gate_y + up_y]
            saved = [(gate_pre, up_pre), tuple(by_core)]
            for s in range(ny - 1):
                saved += [(gate_y[s], up_y[s]), (y_core[s], y_core[ny - 1 + s])]
            act_t = activation(saved, following(terms[2][0]))
            more = [act_t]
        out = join(*over, na, nb, where, *more, *terms[k - 2])
        others[k - 3] = list(out[: len(over)]) if over else others[k - 3]
        a, b, where = out[len(over) : len(over) + 3]
        terms[k - 2], more = list(out[-2:]), list(out[len(over) + 3 : -2])
        if k == 2:
            gate_y, up_y, up_t = more[: ny - 1], more[ny - 1 : -1], more[-1]
        elif k == 3:
            by_core = more
        elif k == 4:
            act_t = more[0]
    far, in_t = join(a, in_t)
    ia, ib = from_ahead(in_t), from_behind(in_t)
    chip = chip_sum(half - 2)
    others[half - 2] = spread_y(chip)
    hidden(last, grad_out, far, following(chip))
    after = following(terms[last][0])
    for n in range(half - 2):
        grads(n, after)
        after = following(own[n])
    ia, ib, where, own[half - 3], *rest = join(ia, ib, where, own[half - 3], *others[half - 2])
    others[half - 2] = rest
    in_pairs = [(ia, ib)]

    ia, ib = from_ahead(ia), from_behind(ib)
    chip = chip_sum(last)
    others[last], after = spread_y(chip), following(chip)
    for n in range(half - 2):
        got[n] = swap_core(own[n])
    grad_down = weight_grad(act_t, go_rows, mask_down, after, places=half)
    ia, ib, where, grad_down, *rest = join(ia, ib, where, grad_down, *others[last])
    others[last] = rest
    in_pairs.append((ia, ib))

    for _ in range(2, half - 1):
        ia, ib = from_ahead(ia), from_behind(ib)
        in_pairs.append((ia, ib))
    grads(last, where)
    got[last] = swap_core(own[last])
    grads(half - 2, following(own[last]))
    got[half - 2] = swap_core(own[half - 2])

    def part(ns, after):
        rows = [x for n in ns for x in (own[n], got[n])]
        return input_part(rows, gate_t, up_t, after)

    both = part([last], following(own[half - 2]))
    to_self = jnp.where(first, both[0], both[1])
    to_far = jnp.where(first, both[1], both[0]).astype(BF16)
    to_far, ia, where = join(to_far, ia, where)

    run_a, run_b, in_far = from_behind(to_far), None, from_ahead(ia)
    parts[half - 2] = part([half - 2], where)
    run_a, where, parts[half - 2] = join(run_a, where, parts[half - 2])

    def send_sums(d):
        add_a = parts[d - 1][0] + run_a.astype(F32)
        add_b = parts[d - 1][1] + run_b.astype(F32) if run_b is not None else parts[d - 1][1]
        return from_behind(add_a.astype(BF16)), from_ahead(add_b.astype(BF16))

    run_a, run_b = send_sums(half - 1)
    both = part(list(range(half - 2)), where)
    lefts = [x for pair in in_pairs for x in pair]
    lefts += [jnp.where(first, in_t, in_far), jnp.where(first, in_far, in_t)]
    rights = [x for n in range(half) for x in (own[n], got[n])]
    run_a, run_b, where, both, *lefts = join(run_a, run_b, where, both, *lefts)
    for n in range(half - 2):
        parts[n] = both[2 * n : 2 * n + 2]

    grad_gate = grad_up = None
    for d in range(half - 2, 0, -1):
        run_a, run_b = send_sums(d)
        if d == half - 2:
            grad_gate = weight_grad(lefts, rights, mask_gate, where, 0)
            run_a, run_b, where, grad_gate = join(run_a, run_b, where, grad_gate)
        elif d == half - 3:
            grad_up = weight_grad(lefts, rights, mask_up, where, 1)
    grad_inputs = (to_self + run_a.astype(F32) + run_b.astype(F32)).astype(BF16)
    return (grad_inputs, grad_gate, grad_up, grad_down)


def solution(mesh):
    placed = (
        P("col", "row"),
        P("col", "row"),
        P("row", "col"),
        P("row", "col"),
        P("row", "col"),
        P("row", "col"),
        P("col", "row"),
        P("row", "col"),
        P("row", "col"),
        P("col", "row"),
    )
    return jax.shard_map(
        functools.partial(per_device, mesh.shape["row"], mesh.shape["col"]),
        mesh=mesh,
        in_specs=placed,
        out_specs=(P("col", "row"), P("row", "col"), P("row", "col"), P("col", "row")),
        check_vma=False,
    )
```

```python
import functools

import jax
import jax.numpy as jnp
from jax import lax
from jax.experimental import pallas as pl
from jax.experimental.pallas import tpu as pltpu
from jax.sharding import PartitionSpec as P

F32 = jnp.float32
BF16 = jnp.bfloat16
MIB = 1024 * 1024
NT = (((1,), (1,)), ((), ()))
NN = (((1,), (0,)), ((), ()))


def params(mib):
    return pltpu.CompilerParams(vmem_limit_bytes=mib * MIB)


def cost(flops, nbytes):
    return pl.CostEstimate(flops=flops // 4096, bytes_accessed=nbytes // 4096, transcendentals=0)


def smem_spec():
    return pl.BlockSpec(memory_space=pltpu.SMEM)


def whole_spec(x):
    return pl.BlockSpec(x.shape, lambda *_: (0,) * x.ndim, pipeline_mode=pl.Buffered(1))


def in_hbm(x):
    return pltpu.with_memory_space_constraint(x, pltpu.HBM)


def stack_rows(dst_ref, refs):
    at = 0
    for r in refs:
        dst_ref[at : at + r.shape[0]] = r[...]
        at += r.shape[0]


def tile_copy(w_ref, dst_ref, sem_ref, t):
    rows = dst_ref.shape[1]
    at = pl.ds(pl.multiple_of(t * rows, rows), rows)
    return pltpu.make_async_copy(w_ref.at[at], dst_ref.at[t], sem_ref.at[t])


def apply_mask(dst_ref, w_ref, m_ref, i, blk):
    for a in range(2):
        for j in range(w_ref.shape[1] // blk):
            keep = m_ref[2 * i + a, j].astype(F32).astype(BF16)
            ra, cj = slice(a * blk, (a + 1) * blk), slice(j * blk, (j + 1) * blk)
            dst_ref[ra, cj] = w_ref[ra, cj] * keep


def hidden_part(where, first, second, w, mask, swap):
    h, d = w.shape
    blk = h // mask.shape[0]
    m = first.shape[0]
    tile = 2 * blk

    def body(at_ref, m_ref, w_ref, a_ref, b_ref, keep_ref, send_ref, rows_ref, eff_ref, all_ref, sem_ref):
        j = pl.program_id(0)

        @pl.when(j == 0)
        def _():
            for t in range(h // tile):
                tile_copy(w_ref, all_ref, sem_ref, t).start()
            stack_rows(rows_ref, (a_ref, b_ref))

        tile_copy(w_ref, all_ref, sem_ref, j).wait()
        apply_mask(eff_ref, all_ref.at[j], m_ref, j, blk)
        out = lax.dot_general(rows_ref[...], eff_ref[...], NT, preferred_element_type=F32)
        one, two = out[:m], out[m:]
        if swap:
            here = at_ref[where.shape[0] - 1] == 0
            one, two = jnp.where(here, one, two), jnp.where(here, two, one)
        keep_ref[...] = one
        send_ref[...] = two.astype(BF16)

    out_spec = pl.BlockSpec((m, tile), lambda j: (0, j))
    return pl.pallas_call(
        body,
        grid=(h // tile,),
        in_specs=[
            smem_spec(),
            smem_spec(),
            pl.BlockSpec(memory_space=pl.ANY),
            whole_spec(first),
            whole_spec(second),
        ],
        out_specs=[out_spec, out_spec],
        out_shape=[jax.ShapeDtypeStruct((m, h), F32), jax.ShapeDtypeStruct((m, h), BF16)],
        scratch_shapes=[
            pltpu.VMEM((2 * m, d), BF16),
            pltpu.VMEM((tile, d), BF16),
            pltpu.VMEM((h // tile, tile, d), BF16),
            pltpu.SemaphoreType.DMA((h // tile,)),
        ],
        compiler_params=params(16),
        cost_estimate=cost(4 * m * d * h, 2 * d * (m + h) + 6 * m * h),
        name="hidden_part",
    )(where, mask, in_hbm(w), first, second)


def activation(saved, where):
    m, h = saved[0][0].shape
    n = len(saved)
    wide = 256 if h % 256 == 0 else 128

    def body(at_ref, *refs):
        o_ref, buf_ref, sem_ref = refs[2 * n :]
        k = pl.program_id(0)

        def copy(src, i, p):
            return pltpu.make_async_copy(refs[2 * src + p], buf_ref.at[i, p], sem_ref.at[i, p])

        @pl.when(k == 0)
        def _():
            for i in range(n):
                for p in range(2):
                    copy(i, i, p).start()

        for p in range(2):
            copy(0, k, p).wait()
        for c in range(h // wide):
            at = slice(c * wide, (c + 1) * wide)
            g = buf_ref[k, 0, :, at].astype(F32)
            u = buf_ref[k, 1, :, at].astype(F32)
            act = g * (1.0 / (1.0 + jnp.exp(-g))) * u
            o_ref[at, :] = act.astype(BF16).T

    return pl.pallas_call(
        body,
        grid=(n,),
        in_specs=[smem_spec()] + [pl.BlockSpec(memory_space=pl.ANY)] * (2 * n),
        out_specs=pl.BlockSpec((h, m), lambda k: (0, k)),
        out_shape=jax.ShapeDtypeStruct((h, n * m), BF16),
        scratch_shapes=[pltpu.VMEM((n, 2, m, h), BF16), pltpu.SemaphoreType.DMA((n, 2))],
        compiler_params=params(16),
        cost_estimate=cost(10 * h * n * m, 6 * h * n * m),
        name="activation",
    )(where, *[in_hbm(x) for pair in saved for x in pair])


def swiglu_grads(sums, saved, where, n, q):
    m, h = sums[0].shape
    cuts = 2 if (h // 2) % 128 == 0 else 1
    wide = h // cuts
    ns, nt = len(saved), len(sums)

    def body(i_ref, *refs):
        s_refs, t_refs = refs[: 2 * ns], refs[2 * ns : 2 * ns + nt]
        o_ref, s_buf = refs[2 * ns + nt], refs[2 * ns + nt + 1]
        t_bufs = refs[2 * ns + nt + 2 : 2 * ns + 2 * nt + 2]
        o_buf, s_sem, t_sem, o_sem = refs[2 * ns + 2 * nt + 2 :]
        src = i_ref[n] // q
        rows = pl.ds(pl.multiple_of(i_ref[n] % q * m, m), m)

        def saved_copy(c, k, p):
            cols = slice(c * wide, (c + 1) * wide)
            return pltpu.make_async_copy(
                s_refs[2 * k + p].at[rows, cols], s_buf.at[c, p], s_sem.at[c, p]
            )

        def term_copy(c, t):
            cols = slice(c * wide, (c + 1) * wide)
            return pltpu.make_async_copy(t_refs[t].at[:, cols], t_bufs[t].at[c], t_sem.at[c, t])

        def out_copy(c):
            cols = slice(c * wide, (c + 1) * wide)
            return pltpu.make_async_copy(o_buf.at[c], o_ref.at[:, :, cols], o_sem.at[c])

        for c in range(cuts):
            for k in range(ns):

                @pl.when(src == k)
                def _():
                    for p in range(2):
                        saved_copy(c, k, p).start()

            for t in range(nt):
                term_copy(c, t).start()
        for c in range(cuts):
            for p in range(2):
                saved_copy(c, 0, p).wait()
            for t in range(nt):
                term_copy(c, t).wait()
            hg = t_bufs[0][c].astype(F32)
            for t in range(1, nt):
                hg = hg + t_bufs[t][c].astype(F32)
            g = s_buf[c, 0].astype(F32)
            u = s_buf[c, 1].astype(F32)
            sig = 1.0 / (1.0 + jnp.exp(-g))
            hs = hg * sig
            o_buf[c, 0] = (hs * u * (1.0 + g * (1.0 - sig))).astype(BF16)
            o_buf[c, 1] = (hs * g).astype(BF16)
            out_copy(c).start()
        for c in range(cuts):
            out_copy(c).wait()

    anywhere = pl.BlockSpec(memory_space=pl.ANY)
    return pl.pallas_call(
        body,
        in_specs=[smem_spec()] + [anywhere] * (2 * ns + nt),
        out_specs=anywhere,
        out_shape=jax.ShapeDtypeStruct((2, m, h), BF16),
        scratch_shapes=[pltpu.VMEM((cuts, 2, m, wide), BF16)]
        + [pltpu.VMEM((cuts, m, wide), x.dtype) for x in sums]
        + [
            pltpu.VMEM((cuts, 2, m, wide), BF16),
            pltpu.SemaphoreType.DMA((cuts, 2)),
            pltpu.SemaphoreType.DMA((cuts, nt)),
            pltpu.SemaphoreType.DMA((cuts,)),
        ],
        compiler_params=params(8),
        cost_estimate=cost(20 * h * m, 14 * h * m),
        name="swiglu_grads",
    )(where, *[in_hbm(x) for pair in saved for x in pair], *sums)


def turned_weight(w, mask, where):
    d, h = w.shape
    nr, nc = mask.shape
    blk = d // nr
    tile = 2 * blk

    def body(at_ref, m_ref, w_ref, o_ref):
        i = pl.program_id(0)
        for j in range(nc):
            cols = slice(j * blk, (j + 1) * blk)
            halves = []
            for a in range(2):
                keep = m_ref[2 * i + a, j].astype(F32).astype(BF16)
                halves.append(w_ref[a * blk : (a + 1) * blk, cols] * keep)
            o_ref[0, cols, :] = jnp.concatenate(halves, 0).T

    return pl.pallas_call(
        body,
        grid=(d // tile,),
        in_specs=[smem_spec(), smem_spec(), pl.BlockSpec((tile, h), lambda i: (i, 0))],
        out_specs=pl.BlockSpec((1, h, tile), lambda i: (i, 0, 0)),
        out_shape=pltpu.HBM((d // tile, h, tile), BF16),
        compiler_params=params(8),
        cost_estimate=cost(d * h, 4 * d * h),
        name="turned_weight",
    )(where, mask, in_hbm(w))


def input_part(grads, gate_t, up_t, where):
    _, m, h = grads[0].shape
    n = len(grads)
    tiles, _, tile = gate_t.shape
    d = tiles * tile

    def body(at_ref, wg_ref, wu_ref, *refs):
        o_ref, g_ref, u_ref, wg_all, wu_all, g_sem, u_sem = refs[n:]
        i = pl.program_id(0)

        def copies(t):
            return (
                pltpu.make_async_copy(wg_ref.at[t], wg_all.at[t], g_sem.at[t]),
                pltpu.make_async_copy(wu_ref.at[t], wu_all.at[t], u_sem.at[t]),
            )

        @pl.when(i == 0)
        def _():
            for t in range(tiles):
                for copy in copies(t):
                    copy.start()
            stack_rows(g_ref, [r.at[0] for r in refs[:n]])
            stack_rows(u_ref, [r.at[1] for r in refs[:n]])

        for copy in copies(i):
            copy.wait()
        out = lax.dot_general(g_ref[...], wg_all[i], NN, preferred_element_type=F32)
        out = out + lax.dot_general(u_ref[...], wu_all[i], NN, preferred_element_type=F32)
        for k in range(n):
            o_ref[k] = out[k * m : (k + 1) * m]

    anywhere = pl.BlockSpec(memory_space=pl.ANY)
    return pl.pallas_call(
        body,
        grid=(tiles,),
        in_specs=[smem_spec(), anywhere, anywhere] + [whole_spec(x) for x in grads],
        out_specs=pl.BlockSpec((n, m, tile), lambda j: (0, 0, j)),
        out_shape=jax.ShapeDtypeStruct((n, m, d), F32),
        scratch_shapes=[pltpu.VMEM((n * m, h), BF16)] * 2
        + [pltpu.VMEM((tiles, h, tile), BF16)] * 2
        + [pltpu.SemaphoreType.DMA((tiles,))] * 2,
        compiler_params=params(28),
        cost_estimate=cost(4 * n * m * d * h, 4 * n * m * h + 4 * d * h + 4 * n * m * d),
        name="input_part",
    )(where, in_hbm(gate_t), in_hbm(up_t), *grads)


def weight_grad(lhs, rhs, mask, where, pick=None, places=None):
    lhs = lhs if isinstance(lhs, list) else [lhs]
    rows = lhs[0].shape[0]
    k = sum(x.shape[1] for x in lhs)
    cols = rhs[0].shape[-1]
    nr, nc = mask.shape
    blk = rows // nr
    per = 4 if nr % 4 == 0 else 2
    tile = per * blk
    wide = 2 * blk
    nl, n = len(lhs), len(rhs)

    def body(m_ref, p_ref, *refs):
        lefts, rights = refs[:nl], refs[nl : nl + n]
        o_ref, r_ref, l_ref = refs[nl + n :]
        i = pl.program_id(0)

        @pl.when(i == 0)
        def _():
            if places is None:
                stack_rows(r_ref, [r if pick is None else r.at[0] for r in rights])
            else:
                for t, r in enumerate(rights):
                    m = r.shape[0]
                    r_ref[pl.ds(pl.multiple_of(p_ref[places + t] * m, m), m)] = r[...]

        if nl > 1:
            at = 0
            for r in lefts:
                l_ref[:, at : at + r.shape[1]] = r[...]
                at += r.shape[1]
        left = l_ref if nl > 1 else lefts[0]
        for c in range(cols // wide):
            out = lax.dot_general(
                left[...], r_ref[:, c * wide : (c + 1) * wide], NN, preferred_element_type=F32
            )
            for a in range(per):
                for s in range(2):
                    keep = m_ref[i * per + a, 2 * c + s].astype(F32)
                    ra, cs = slice(a * blk, (a + 1) * blk), slice(s * blk, (s + 1) * blk)
                    at = slice((2 * c + s) * blk, (2 * c + s + 1) * blk)
                    o_ref[ra, at] = (out[ra, cs] * keep).astype(BF16)

    specs = [pl.BlockSpec((tile, x.shape[1]), lambda i: (i, 0)) for x in lhs]
    for r in rhs:
        if pick is None:
            specs.append(whole_spec(r))
        else:
            specs.append(
                pl.BlockSpec(
                    (1,) + r.shape[1:], lambda i: (pick, 0, 0), pipeline_mode=pl.Buffered(1)
                )
            )
    return pl.pallas_call(
        body,
        grid=(rows // tile,),
        in_specs=[smem_spec(), smem_spec()] + specs,
        out_specs=pl.BlockSpec((tile, cols), lambda i: (i, 0)),
        out_shape=jax.ShapeDtypeStruct((rows, cols), BF16),
        scratch_shapes=[
            pltpu.VMEM((k, cols), BF16),
            pltpu.VMEM((tile, k) if nl > 1 else (16, 128), BF16),
        ],
        compiler_params=params(20),
        cost_estimate=cost(2 * rows * cols * k, 2 * (rows * k + cols * k + rows * cols)),
        name="weight_grad",
    )(mask, where, *lhs, *rhs)


def join(*xs):
    return lax.optimization_barrier(xs)


def ring_order(n):
    a = 4 if n % 4 == 0 and n > 4 else 2
    b = n // a
    walk = [(0, j) for j in range(b)]
    for i in range(1, a):
        js = range(b - 1, 0, -1) if i % 2 else range(1, b)
        walk += [(i, j) for j in js]
    walk += [(i, 0) for i in range(a - 1, 0, -1)]
    return [i * b + j for i, j in walk]


def per_device(
    n_row, n_col, inputs, grad_out, gate_pre, up_pre, w_gate, w_up, w_down, mask_gate, mask_up, mask_down
):
    order = ring_order(n_col)
    half = n_col // 2
    ny = n_row // 2
    tpc = inputs.shape[0]
    q = gate_pre.shape[0] // tpc
    row = lax.axis_index("row")
    core = row % 2
    first = core == 0

    def ring_perm(step):
        pairs = []
        for r in range(n_row):
            s = step if r % 2 == 0 else -step
            for p in range(n_col):
                pairs.append((r * n_col + order[p], r * n_col + order[(p + s) % n_col]))
        return pairs

    back, ahead = ring_perm(-1), ring_perm(1)

    def from_ahead(x):
        return lax.ppermute(x, ("row", "col"), back)

    def from_behind(x):
        return lax.ppermute(x, ("row", "col"), ahead)

    def swap_core(x):
        return lax.ppermute(x, "row", [(r, r ^ 1) for r in range(n_row)])

    def shift_y(x, s):
        return lax.ppermute(
            x, "row", [(r, (r // 2 + s) % ny * 2 + r % 2) for r in range(n_row)]
        )

    last = half - 1
    dists = list(range(1, half)) + [0] + [s * d for d in range(1, half) for s in (1, -1)] + [0, half]
    at = lax.iota(jnp.int32, len(dists) + 1)
    dist = jnp.zeros_like(at)
    for i, d in enumerate(dists):
        if d:
            dist = jnp.where(at == i, d, dist)
    dist = jnp.where(at == last, core * half, dist)
    col = lax.axis_index("col")
    pos = sum(jnp.where(col == c, p, 0) for p, c in enumerate(order))
    near = (pos + (1 - 2 * core) * dist + 2 * n_col) % n_col
    block = sum(jnp.where(near == p, c, 0) for p, c in enumerate(order))
    owner = block // q
    s = (row // 2 - owner // 2 + ny) % ny
    e = (owner % 2 + core) % 2
    where = jnp.where(at == len(dists), core, (s * 2 + e) * q + block % q).astype(jnp.int32)

    def spread_y(x):
        return [shift_y(x, s) for s in range(1, ny)]

    go_rows, terms = [], []
    others, own, got, parts = [None] * half, [None] * half, [None] * half, [None] * half

    def hidden(n, x, y, after):
        kept, sent = hidden_part(after, x, y, w_down, mask_down, n == last)
        go_rows.extend([x, y])
        terms.append([kept, swap_core(sent)])

    def chip_sum(n):
        chip = (terms[n][0] + terms[n][1].astype(F32)).astype(BF16)
        return jnp.pad(chip, ((0, 0), (0, 128)))

    def grads(n, after):
        sums = terms[n] + others[n]
        if n == half - 2:
            sums = [in_hbm(x) for x in sums]
        own[n] = swiglu_grads(sums, saved, after, n, q)

    def following(x):
        return join(where, x)[0]

    a, b = from_ahead(grad_out), from_behind(grad_out)
    gate_y, up_y, in_t = spread_y(gate_pre), spread_y(up_pre), inputs.T
    by_core = []
    gate_t = turned_weight(w_gate, mask_gate, where)
    a, b, where, in_t, gate_t, *by_core = join(a, b, where, in_t, gate_t, *by_core)

    up_t, y_core = None, []
    for k in range(2, half + 1):
        na = from_ahead(a)
        nb = from_behind(b) if k < half else b
        after = where
        if k > 2:
            chip = chip_sum(k - 3)
            after = following(chip)
        hidden(k - 2, a, b, after)
        over, more = [], []
        if k > 2:
            over = others[k - 3] = spread_y(chip)
        if k == 2:
            up_t = turned_weight(w_up, mask_up, following(terms[0][0]))
            more = gate_y + up_y + [up_t]
        elif k == 3:
            by_core = [swap_core(gate_pre)]
            more = by_core
        elif k == 4:
            by_core = by_core + [swap_core(up_pre)]
            y_core = [swap_core(x) for x in gate_y + up_y]
            saved = [(gate_pre, up_pre), tuple(by_core)]
            for s in range(ny - 1):
                saved += [(gate_y[s], up_y[s]), (y_core[s], y_core[ny - 1 + s])]
            act_t = activation(saved, following(terms[2][0]))
            more = [act_t]
        out = join(*over, na, nb, where, *more, *terms[k - 2])
        others[k - 3] = list(out[: len(over)]) if over else others[k - 3]
        a, b, where = out[len(over) : len(over) + 3]
        terms[k - 2], more = list(out[-2:]), list(out[len(over) + 3 : -2])
        if k == 2:
            gate_y, up_y, up_t = more[: ny - 1], more[ny - 1 : -1], more[-1]
        elif k == 3:
            by_core = more
        elif k == 4:
            act_t = more[0]
    far, in_t = join(a, in_t)
    ia, ib = from_ahead(in_t), from_behind(in_t)
    chip = chip_sum(half - 2)
    others[half - 2] = spread_y(chip)
    hidden(last, grad_out, far, following(chip))
    after = following(terms[last][0])
    for n in range(half - 2):
        grads(n, after)
        after = following(own[n])
    ia, ib, where, own[half - 3], *rest = join(ia, ib, where, own[half - 3], *others[half - 2])
    others[half - 2] = rest
    in_pairs = [(ia, ib)]

    ia, ib = from_ahead(ia), from_behind(ib)
    chip = chip_sum(last)
    others[last], after = spread_y(chip), following(chip)
    for n in range(half - 2):
        got[n] = swap_core(own[n])
    grad_down = weight_grad(act_t, go_rows, mask_down, after, places=half)
    ia, ib, where, grad_down, *rest = join(
        ia, ib, where, grad_down, *others[last], *got[: half - 2]
    )
    others[last], got[: half - 2] = rest[: ny - 1], rest[ny - 1 :]
    in_pairs.append((ia, ib))

    for _ in range(2, half - 1):
        ia, ib = from_ahead(ia), from_behind(ib)
        in_pairs.append((ia, ib))
    grads(last, where)
    got[last] = swap_core(own[last])
    grads(half - 2, following(own[last]))
    got[half - 2] = swap_core(own[half - 2])

    def part(ns, after):
        rows = [x for n in ns for x in (own[n], got[n])]
        return input_part(rows, gate_t, up_t, after)

    both = part([last], following(own[half - 2]))
    to_self = jnp.where(first, both[0], both[1])
    to_far = jnp.where(first, both[1], both[0]).astype(BF16)
    to_far, where, *early = join(to_far, where, *in_pairs[-1], *got[: half - 2])
    in_pairs[-1] = tuple(early[:2])
    got[: half - 2] = early[2:]
    ia = in_pairs[-1][0]

    run_a, run_b, in_far = from_behind(to_far), None, from_ahead(ia)
    parts[half - 2] = part([half - 2], where)
    run_a, where, parts[half - 2] = join(run_a, where, parts[half - 2])

    def send_sums(d):
        add_a = parts[d - 1][0] + run_a.astype(F32)
        add_b = parts[d - 1][1] + run_b.astype(F32) if run_b is not None else parts[d - 1][1]
        return from_behind(add_a.astype(BF16)), from_ahead(add_b.astype(BF16))

    run_a, run_b = send_sums(half - 1)
    both = part(list(range(half - 2)), where)
    lefts = [x for pair in in_pairs for x in pair]
    lefts += [jnp.where(first, in_t, in_far), jnp.where(first, in_far, in_t)]
    rights = [x for n in range(half) for x in (own[n], got[n])]
    run_a, run_b, where, both, *lefts = join(run_a, run_b, where, both, *lefts)
    for n in range(half - 2):
        parts[n] = both[2 * n : 2 * n + 2]

    grad_gate = grad_up = None
    for d in range(half - 2, 0, -1):
        run_a, run_b = send_sums(d)
        if d == half - 2:
            grad_gate = weight_grad(lefts, rights, mask_gate, where, 0)
            run_a, run_b, where, grad_gate = join(run_a, run_b, where, grad_gate)
        elif d == half - 3:
            grad_up = weight_grad(lefts, rights, mask_up, where, 1)
    grad_inputs = (to_self + run_a.astype(F32) + run_b.astype(F32)).astype(BF16)
    return (grad_inputs, grad_gate, grad_up, grad_down)


def solution(mesh):
    placed = (
        P("col", "row"),
        P("col", "row"),
        P("row", "col"),
        P("row", "col"),
        P("row", "col"),
        P("row", "col"),
        P("col", "row"),
        P("row", "col"),
        P("row", "col"),
        P("col", "row"),
    )
    return jax.shard_map(
        functools.partial(per_device, mesh.shape["row"], mesh.shape["col"]),
        mesh=mesh,
        in_specs=placed,
        out_specs=(P("col", "row"), P("row", "col"), P("row", "col"), P("col", "row")),
        check_vma=False,
    )
```

```python
import functools

import jax
import jax.numpy as jnp
from jax import lax
from jax.experimental import pallas as pl
from jax.experimental.pallas import tpu as pltpu
from jax.sharding import PartitionSpec as P

F32 = jnp.float32
BF16 = jnp.bfloat16
MIB = 1024 * 1024
NT = (((1,), (1,)), ((), ()))
NN = (((1,), (0,)), ((), ()))


def params(mib):
    return pltpu.CompilerParams(vmem_limit_bytes=mib * MIB)


def cost(flops, nbytes):
    return pl.CostEstimate(flops=flops // 4096, bytes_accessed=nbytes // 4096, transcendentals=0)


def smem_spec():
    return pl.BlockSpec(memory_space=pltpu.SMEM)


def whole_spec(x):
    return pl.BlockSpec(x.shape, lambda *_: (0,) * x.ndim, pipeline_mode=pl.Buffered(1))


def in_hbm(x):
    return pltpu.with_memory_space_constraint(x, pltpu.HBM)


def stack_rows(dst_ref, refs):
    at = 0
    for r in refs:
        dst_ref[at : at + r.shape[0]] = r[...]
        at += r.shape[0]


def tile_copy(w_ref, dst_ref, sem_ref, t):
    rows = dst_ref.shape[1]
    at = pl.ds(pl.multiple_of(t * rows, rows), rows)
    return pltpu.make_async_copy(w_ref.at[at], dst_ref.at[t], sem_ref.at[t])


def apply_mask(dst_ref, w_ref, m_ref, i, blk):
    for a in range(2):
        for j in range(w_ref.shape[1] // blk):
            keep = m_ref[2 * i + a, j].astype(F32).astype(BF16)
            ra, cj = slice(a * blk, (a + 1) * blk), slice(j * blk, (j + 1) * blk)
            dst_ref[ra, cj] = w_ref[ra, cj] * keep


def hidden_part(where, first, second, w, mask, swap):
    h, d = w.shape
    blk = h // mask.shape[0]
    m = first.shape[0]
    tile = 2 * blk

    def body(at_ref, m_ref, w_ref, a_ref, b_ref, keep_ref, send_ref, rows_ref, eff_ref, all_ref, sem_ref):
        j = pl.program_id(0)

        @pl.when(j == 0)
        def _():
            for t in range(h // tile):
                tile_copy(w_ref, all_ref, sem_ref, t).start()
            stack_rows(rows_ref, (a_ref, b_ref))

        tile_copy(w_ref, all_ref, sem_ref, j).wait()
        apply_mask(eff_ref, all_ref.at[j], m_ref, j, blk)
        out = lax.dot_general(rows_ref[...], eff_ref[...], NT, preferred_element_type=F32)
        one, two = out[:m], out[m:]
        if swap:
            here = at_ref[where.shape[0] - 1] == 0
            one, two = jnp.where(here, one, two), jnp.where(here, two, one)
        keep_ref[...] = one
        send_ref[...] = two.astype(BF16)

    out_spec = pl.BlockSpec((m, tile), lambda j: (0, j))
    return pl.pallas_call(
        body,
        grid=(h // tile,),
        in_specs=[
            smem_spec(),
            smem_spec(),
            pl.BlockSpec(memory_space=pl.ANY),
            whole_spec(first),
            whole_spec(second),
        ],
        out_specs=[out_spec, out_spec],
        out_shape=[jax.ShapeDtypeStruct((m, h), F32), jax.ShapeDtypeStruct((m, h), BF16)],
        scratch_shapes=[
            pltpu.VMEM((2 * m, d), BF16),
            pltpu.VMEM((tile, d), BF16),
            pltpu.VMEM((h // tile, tile, d), BF16),
            pltpu.SemaphoreType.DMA((h // tile,)),
        ],
        compiler_params=params(16),
        cost_estimate=cost(4 * m * d * h, 2 * d * (m + h) + 6 * m * h),
        name="hidden_part",
    )(where, mask, in_hbm(w), first, second)


def activation(saved, where):
    m, h = saved[0][0].shape
    n = len(saved)
    wide = 256 if h % 256 == 0 else 128

    def body(at_ref, *refs):
        o_ref, buf_ref, sem_ref = refs[2 * n :]
        k = pl.program_id(0)

        def copy(src, i, p):
            return pltpu.make_async_copy(refs[2 * src + p], buf_ref.at[i, p], sem_ref.at[i, p])

        @pl.when(k == 0)
        def _():
            for i in range(n):
                for p in range(2):
                    copy(i, i, p).start()

        for p in range(2):
            copy(0, k, p).wait()
        for c in range(h // wide):
            at = slice(c * wide, (c + 1) * wide)
            g = buf_ref[k, 0, :, at].astype(F32)
            u = buf_ref[k, 1, :, at].astype(F32)
            act = g * (1.0 / (1.0 + jnp.exp(-g))) * u
            o_ref[at, :] = act.astype(BF16).T

    return pl.pallas_call(
        body,
        grid=(n,),
        in_specs=[smem_spec()] + [pl.BlockSpec(memory_space=pl.ANY)] * (2 * n),
        out_specs=pl.BlockSpec((h, m), lambda k: (0, k)),
        out_shape=jax.ShapeDtypeStruct((h, n * m), BF16),
        scratch_shapes=[pltpu.VMEM((n, 2, m, h), BF16), pltpu.SemaphoreType.DMA((n, 2))],
        compiler_params=params(16),
        cost_estimate=cost(10 * h * n * m, 6 * h * n * m),
        name="activation",
    )(where, *[in_hbm(x) for pair in saved for x in pair])


def swiglu_grads(sums, saved, where, n, q):
    m, h = sums[0].shape
    wide = 256 if h % 256 == 0 else 128
    cuts = h // wide
    ns, nt = len(saved), len(sums)

    def body(i_ref, *refs):
        s_refs, t_refs = refs[: 2 * ns], refs[2 * ns : 2 * ns + nt]
        o_ref, s_buf = refs[2 * ns + nt], refs[2 * ns + nt + 1]
        t_bufs = refs[2 * ns + nt + 2 : 2 * ns + 2 * nt + 2]
        o_buf, s_sem, t_sem, o_sem = refs[2 * ns + 2 * nt + 2 :]
        src = i_ref[n] // q
        rows = pl.ds(pl.multiple_of(i_ref[n] % q * m, m), m)

        def saved_copy(c, k, p):
            cols = slice(c * wide, (c + 1) * wide)
            return pltpu.make_async_copy(
                s_refs[2 * k + p].at[rows, cols], s_buf.at[c, p], s_sem.at[c, p]
            )

        def term_copy(c, t):
            cols = slice(c * wide, (c + 1) * wide)
            return pltpu.make_async_copy(t_refs[t].at[:, cols], t_bufs[t].at[c], t_sem.at[c, t])

        def out_copy(c):
            cols = slice(c * wide, (c + 1) * wide)
            return pltpu.make_async_copy(o_buf.at[c], o_ref.at[:, :, cols], o_sem.at[c])

        for c in range(cuts):
            for k in range(ns):

                @pl.when(src == k)
                def _():
                    for p in range(2):
                        saved_copy(c, k, p).start()

            for t in range(nt):
                term_copy(c, t).start()
        for c in range(cuts):
            for p in range(2):
                saved_copy(c, 0, p).wait()
            for t in range(nt):
                term_copy(c, t).wait()
            hg = t_bufs[0][c].astype(F32)
            for t in range(1, nt):
                hg = hg + t_bufs[t][c].astype(F32)
            g = s_buf[c, 0].astype(F32)
            u = s_buf[c, 1].astype(F32)
            sig = 1.0 / (1.0 + jnp.exp(-g))
            hs = hg * sig
            o_buf[c, 0] = (hs * u * (1.0 + g * (1.0 - sig))).astype(BF16)
            o_buf[c, 1] = (hs * g).astype(BF16)
            out_copy(c).start()
        for c in range(cuts):
            out_copy(c).wait()

    anywhere = pl.BlockSpec(memory_space=pl.ANY)
    return pl.pallas_call(
        body,
        in_specs=[smem_spec()] + [anywhere] * (2 * ns + nt),
        out_specs=anywhere,
        out_shape=jax.ShapeDtypeStruct((2, m, h), BF16),
        scratch_shapes=[pltpu.VMEM((cuts, 2, m, wide), BF16)]
        + [pltpu.VMEM((cuts, m, wide), x.dtype) for x in sums]
        + [
            pltpu.VMEM((cuts, 2, m, wide), BF16),
            pltpu.SemaphoreType.DMA((cuts, 2)),
            pltpu.SemaphoreType.DMA((cuts, nt)),
            pltpu.SemaphoreType.DMA((cuts,)),
        ],
        compiler_params=params(8),
        cost_estimate=cost(20 * h * m, 14 * h * m),
        name="swiglu_grads",
    )(where, *[in_hbm(x) for pair in saved for x in pair], *sums)


def turned_weight(w, mask, where):
    d, h = w.shape
    nr, nc = mask.shape
    blk = d // nr
    tile = 2 * blk

    def body(at_ref, m_ref, w_ref, o_ref):
        i = pl.program_id(0)
        for j in range(nc):
            cols = slice(j * blk, (j + 1) * blk)
            halves = []
            for a in range(2):
                keep = m_ref[2 * i + a, j].astype(F32).astype(BF16)
                halves.append(w_ref[a * blk : (a + 1) * blk, cols] * keep)
            o_ref[0, cols, :] = jnp.concatenate(halves, 0).T

    return pl.pallas_call(
        body,
        grid=(d // tile,),
        in_specs=[smem_spec(), smem_spec(), pl.BlockSpec((tile, h), lambda i: (i, 0))],
        out_specs=pl.BlockSpec((1, h, tile), lambda i: (i, 0, 0)),
        out_shape=pltpu.HBM((d // tile, h, tile), BF16),
        compiler_params=params(8),
        cost_estimate=cost(d * h, 4 * d * h),
        name="turned_weight",
    )(where, mask, in_hbm(w))


def input_part(grads, gate_t, up_t, where):
    _, m, h = grads[0].shape
    n = len(grads)
    tiles, _, tile = gate_t.shape
    d = tiles * tile

    def body(at_ref, wg_ref, wu_ref, *refs):
        o_ref, g_ref, u_ref, wg_all, wu_all, g_sem, u_sem = refs[n:]
        i = pl.program_id(0)

        def copies(t):
            return (
                pltpu.make_async_copy(wg_ref.at[t], wg_all.at[t], g_sem.at[t]),
                pltpu.make_async_copy(wu_ref.at[t], wu_all.at[t], u_sem.at[t]),
            )

        @pl.when(i == 0)
        def _():
            for t in range(tiles):
                for copy in copies(t):
                    copy.start()
            stack_rows(g_ref, [r.at[0] for r in refs[:n]])
            stack_rows(u_ref, [r.at[1] for r in refs[:n]])

        for copy in copies(i):
            copy.wait()
        out = lax.dot_general(g_ref[...], wg_all[i], NN, preferred_element_type=F32)
        out = out + lax.dot_general(u_ref[...], wu_all[i], NN, preferred_element_type=F32)
        for k in range(n):
            o_ref[k] = out[k * m : (k + 1) * m]

    anywhere = pl.BlockSpec(memory_space=pl.ANY)
    return pl.pallas_call(
        body,
        grid=(tiles,),
        in_specs=[smem_spec(), anywhere, anywhere] + [whole_spec(x) for x in grads],
        out_specs=pl.BlockSpec((n, m, tile), lambda j: (0, 0, j)),
        out_shape=jax.ShapeDtypeStruct((n, m, d), F32),
        scratch_shapes=[pltpu.VMEM((n * m, h), BF16)] * 2
        + [pltpu.VMEM((tiles, h, tile), BF16)] * 2
        + [pltpu.SemaphoreType.DMA((tiles,))] * 2,
        compiler_params=params(28),
        cost_estimate=cost(4 * n * m * d * h, 4 * n * m * h + 4 * d * h + 4 * n * m * d),
        name="input_part",
    )(where, in_hbm(gate_t), in_hbm(up_t), *grads)


def weight_grad(lhs, rhs, mask, where, pick=None, places=None):
    lhs = lhs if isinstance(lhs, list) else [lhs]
    rows = lhs[0].shape[0]
    k = sum(x.shape[1] for x in lhs)
    cols = rhs[0].shape[-1]
    nr, nc = mask.shape
    blk = rows // nr
    per = 4 if nr % 4 == 0 else 2
    tile = per * blk
    tiles = rows // tile
    wide = 2 * blk
    nl, n = len(lhs), len(rhs)

    def body(m_ref, p_ref, *refs):
        lefts, rights = refs[:nl], refs[nl : nl + n]
        o_ref, r_ref, l_ref, l_sem, r_sem = refs[nl + n :]
        i = pl.program_id(0)

        def left_copies(t):
            at, out = 0, []
            src = pl.ds(pl.multiple_of(t * tile, tile), tile)
            for j, x in enumerate(lefts):
                dst = l_ref.at[t, :, at : at + x.shape[1]]
                out.append(pltpu.make_async_copy(x.at[src], dst, l_sem.at[t, j]))
                at += x.shape[1]
            return out

        def right_copies():
            at, out = 0, []
            for t, x in enumerate(rights):
                x = x if pick is None else x.at[pick]
                m = x.shape[0]
                if places is None:
                    dst = r_ref.at[at : at + m]
                else:
                    dst = r_ref.at[pl.ds(pl.multiple_of(p_ref[places + t] * m, m), m)]
                out.append(pltpu.make_async_copy(x, dst, r_sem.at[t]))
                at += m
            return out

        @pl.when(i == 0)
        def _():
            first = left_copies(0) + right_copies()
            for copy in first:
                copy.start()
            for copy in first:
                copy.wait()

        @pl.when(i > 0)
        def _():
            for copy in left_copies(i):
                copy.wait()

        @pl.when(i + 1 < tiles)
        def _():
            for copy in left_copies(i + 1):
                copy.start()

        for c in range(cols // wide):
            out = lax.dot_general(
                l_ref[i], r_ref[:, c * wide : (c + 1) * wide], NN, preferred_element_type=F32
            )
            for a in range(per):
                for s in range(2):
                    keep = m_ref[i * per + a, 2 * c + s].astype(F32)
                    ra, cs = slice(a * blk, (a + 1) * blk), slice(s * blk, (s + 1) * blk)
                    at = slice((2 * c + s) * blk, (2 * c + s + 1) * blk)
                    o_ref[ra, at] = (out[ra, cs] * keep).astype(BF16)

    return pl.pallas_call(
        body,
        grid=(tiles,),
        in_specs=[smem_spec(), smem_spec()] + [pl.BlockSpec(memory_space=pl.ANY)] * (nl + n),
        out_specs=pl.BlockSpec((tile, cols), lambda i: (i, 0)),
        out_shape=jax.ShapeDtypeStruct((rows, cols), BF16),
        scratch_shapes=[
            pltpu.VMEM((k, cols), BF16),
            pltpu.VMEM((tiles, tile, k), BF16),
            pltpu.SemaphoreType.DMA((tiles, nl)),
            pltpu.SemaphoreType.DMA((n,)),
        ],
        compiler_params=params(20),
        cost_estimate=cost(2 * rows * cols * k, 2 * (rows * k + cols * k + rows * cols)),
        name="weight_grad",
    )(mask, where, *lhs, *rhs)


def join(*xs):
    return lax.optimization_barrier(xs)


def ring_order(n):
    a = 4 if n % 4 == 0 and n > 4 else 2
    b = n // a
    walk = [(0, j) for j in range(b)]
    for i in range(1, a):
        js = range(b - 1, 0, -1) if i % 2 else range(1, b)
        walk += [(i, j) for j in js]
    walk += [(i, 0) for i in range(a - 1, 0, -1)]
    return [i * b + j for i, j in walk]


def per_device(
    n_row, n_col, inputs, grad_out, gate_pre, up_pre, w_gate, w_up, w_down, mask_gate, mask_up, mask_down
):
    order = ring_order(n_col)
    half = n_col // 2
    ny = n_row // 2
    tpc = inputs.shape[0]
    q = gate_pre.shape[0] // tpc
    row = lax.axis_index("row")
    core = row % 2
    first = core == 0

    def ring_perm(step):
        pairs = []
        for r in range(n_row):
            s = step if r % 2 == 0 else -step
            for p in range(n_col):
                pairs.append((r * n_col + order[p], r * n_col + order[(p + s) % n_col]))
        return pairs

    back, ahead = ring_perm(-1), ring_perm(1)

    def from_ahead(x):
        return lax.ppermute(x, ("row", "col"), back)

    def from_behind(x):
        return lax.ppermute(x, ("row", "col"), ahead)

    def swap_core(x):
        return lax.ppermute(x, "row", [(r, r ^ 1) for r in range(n_row)])

    def shift_y(x, s):
        return lax.ppermute(
            x, "row", [(r, (r // 2 + s) % ny * 2 + r % 2) for r in range(n_row)]
        )

    last = half - 1
    dists = list(range(1, half)) + [0] + [s * d for d in range(1, half) for s in (1, -1)] + [0, half]
    at = lax.iota(jnp.int32, len(dists) + 1)
    dist = jnp.zeros_like(at)
    for i, d in enumerate(dists):
        if d:
            dist = jnp.where(at == i, d, dist)
    dist = jnp.where(at == last, core * half, dist)
    col = lax.axis_index("col")
    pos = sum(jnp.where(col == c, p, 0) for p, c in enumerate(order))
    near = (pos + (1 - 2 * core) * dist + 2 * n_col) % n_col
    block = sum(jnp.where(near == p, c, 0) for p, c in enumerate(order))
    owner = block // q
    s = (row // 2 - owner // 2 + ny) % ny
    e = (owner % 2 + core) % 2
    where = jnp.where(at == len(dists), core, (s * 2 + e) * q + block % q).astype(jnp.int32)

    def spread_y(x):
        return [shift_y(x, s) for s in range(1, ny)]

    go_rows, terms = [], []
    others, own, got, parts = [None] * half, [None] * half, [None] * half, [None] * half

    def hidden(n, x, y, after):
        kept, sent = hidden_part(after, x, y, w_down, mask_down, n == last)
        go_rows.extend([x, y])
        terms.append([kept, swap_core(sent)])

    def chip_sum(n):
        chip = (terms[n][0] + terms[n][1].astype(F32)).astype(BF16)
        return chip if n == last else jnp.pad(chip, ((0, 0), (0, 128)))

    def grads(n, after):
        sums = terms[n] + others[n]
        if n == half - 2:
            sums = [in_hbm(x) for x in sums]
        own[n] = swiglu_grads(sums, saved, after, n, q)

    def following(x):
        return join(where, x)[0]

    a, b = from_ahead(grad_out), from_behind(grad_out)
    gate_y, up_y, in_t = spread_y(gate_pre), spread_y(up_pre), inputs.T
    by_core = []
    gate_t = turned_weight(w_gate, mask_gate, where)
    a, b, where, in_t, gate_t, *by_core = join(a, b, where, in_t, gate_t, *by_core)

    up_t, y_core = None, []
    for k in range(2, half + 1):
        na = from_ahead(a)
        nb = from_behind(b) if k < half else b
        after = where
        if k > 2:
            chip = chip_sum(k - 3)
            after = following(chip)
        hidden(k - 2, a, b, after)
        over, more = [], []
        if k > 2:
            over = others[k - 3] = spread_y(chip)
        if k == 2:
            up_t = turned_weight(w_up, mask_up, following(terms[0][0]))
            more = gate_y + up_y + [up_t]
        elif k == 3:
            by_core = [swap_core(gate_pre)]
            more = by_core
        elif k == 4:
            by_core = by_core + [swap_core(up_pre)]
            y_core = [swap_core(x) for x in gate_y + up_y]
            saved = [(gate_pre, up_pre), tuple(by_core)]
            for s in range(ny - 1):
                saved += [(gate_y[s], up_y[s]), (y_core[s], y_core[ny - 1 + s])]
            act_t = activation(saved, following(terms[2][0]))
            more = [act_t]
        out = join(*over, na, nb, where, *more, *terms[k - 2])
        others[k - 3] = list(out[: len(over)]) if over else others[k - 3]
        a, b, where = out[len(over) : len(over) + 3]
        terms[k - 2], more = list(out[-2:]), list(out[len(over) + 3 : -2])
        if k == 2:
            gate_y, up_y, up_t = more[: ny - 1], more[ny - 1 : -1], more[-1]
        elif k == 3:
            by_core = more
        elif k == 4:
            act_t = more[0]
    far, in_t = join(a, in_t)
    ia, ib = from_ahead(in_t), from_behind(in_t)
    chip = chip_sum(half - 2)
    others[half - 2] = spread_y(chip)
    hidden(last, grad_out, far, following(chip))
    after = following(terms[last][0])
    for n in range(half - 2):
        grads(n, after)
        after = following(own[n])
    ia, ib, where, own[half - 3], *rest = join(ia, ib, where, own[half - 3], *others[half - 2])
    others[half - 2] = rest
    in_pairs = [(ia, ib)]

    ia, ib = from_ahead(ia), from_behind(ib)
    chip = chip_sum(last)
    others[last], after = spread_y(chip), following(chip)
    for n in range(half - 2):
        got[n] = swap_core(own[n])
    grad_down = weight_grad(act_t, go_rows, mask_down, after, places=half)
    ia, ib, where, grad_down, *rest = join(
        ia, ib, where, grad_down, *others[last], *got[: half - 2]
    )
    others[last], got[: half - 2] = rest[: ny - 1], rest[ny - 1 :]
    in_pairs.append((ia, ib))

    for _ in range(2, half - 1):
        ia, ib = from_ahead(ia), from_behind(ib)
        in_pairs.append((ia, ib))
    grads(last, where)
    got[last] = swap_core(own[last])
    grads(half - 2, following(own[last]))
    got[half - 2] = swap_core(own[half - 2])

    def part(ns, after):
        rows = [x for n in ns for x in (own[n], got[n])]
        return input_part(rows, gate_t, up_t, after)

    both = part([last], following(own[half - 2]))
    to_self = jnp.where(first, both[0], both[1])
    to_far = jnp.where(first, both[1], both[0]).astype(BF16)
    to_far, where, *early = join(to_far, where, *in_pairs[-1], *got[: half - 2])
    in_pairs[-1] = tuple(early[:2])
    got[: half - 2] = early[2:]
    ia = in_pairs[-1][0]

    run_a, run_b, in_far = from_behind(to_far), None, from_ahead(ia)
    parts[half - 2] = part([half - 2], where)
    run_a, where, parts[half - 2] = join(run_a, where, parts[half - 2])

    def send_sums(d):
        add_a = parts[d - 1][0] + run_a.astype(F32)
        add_b = parts[d - 1][1] + run_b.astype(F32) if run_b is not None else parts[d - 1][1]
        return from_behind(add_a.astype(BF16)), from_ahead(add_b.astype(BF16))

    run_a, run_b = send_sums(half - 1)
    both = part(list(range(half - 2)), where)
    lefts = [x for pair in in_pairs for x in pair]
    lefts += [jnp.where(first, in_t, in_far), jnp.where(first, in_far, in_t)]
    rights = [x for n in range(half) for x in (own[n], got[n])]
    run_a, run_b, where, both, *lefts = join(run_a, run_b, where, both, *lefts)
    for n in range(half - 2):
        parts[n] = both[2 * n : 2 * n + 2]

    grad_gate = grad_up = None
    for d in range(half - 2, 0, -1):
        run_a, run_b = send_sums(d)
        if d == half - 2:
            grad_gate = weight_grad(lefts, rights, mask_gate, where, 0)
            run_a, run_b, where, grad_gate = join(run_a, run_b, where, grad_gate)
        elif d == half - 3:
            grad_up = weight_grad(lefts, rights, mask_up, where, 1)
    grad_inputs = (to_self + run_a.astype(F32) + run_b.astype(F32)).astype(BF16)
    return (grad_inputs, grad_gate, grad_up, grad_down)


def solution(mesh):
    placed = (
        P("col", "row"),
        P("col", "row"),
        P("row", "col"),
        P("row", "col"),
        P("row", "col"),
        P("row", "col"),
        P("col", "row"),
        P("row", "col"),
        P("row", "col"),
        P("col", "row"),
    )
    return jax.shard_map(
        functools.partial(per_device, mesh.shape["row"], mesh.shape["col"]),
        mesh=mesh,
        in_specs=placed,
        out_specs=(P("col", "row"), P("row", "col"), P("row", "col"), P("col", "row")),
        check_vma=False,
    )
```

```python
import functools

import jax
import jax.numpy as jnp
from jax import lax
from jax.experimental import pallas as pl
from jax.experimental.pallas import tpu as pltpu
from jax.sharding import PartitionSpec as P

F32 = jnp.float32
BF16 = jnp.bfloat16
MIB = 1024 * 1024
NT = (((1,), (1,)), ((), ()))
NN = (((1,), (0,)), ((), ()))


def params(mib):
    return pltpu.CompilerParams(vmem_limit_bytes=mib * MIB)


def cost(flops, nbytes):
    return pl.CostEstimate(flops=flops // 4096, bytes_accessed=nbytes // 4096, transcendentals=0)


def smem_spec():
    return pl.BlockSpec(memory_space=pltpu.SMEM)


def whole_spec(x):
    return pl.BlockSpec(x.shape, lambda *_: (0,) * x.ndim, pipeline_mode=pl.Buffered(1))


def in_hbm(x):
    return pltpu.with_memory_space_constraint(x, pltpu.HBM)


def stack_rows(dst_ref, refs):
    at = 0
    for r in refs:
        dst_ref[at : at + r.shape[0]] = r[...]
        at += r.shape[0]


def tile_copy(w_ref, dst_ref, sem_ref, t):
    rows = dst_ref.shape[1]
    at = pl.ds(pl.multiple_of(t * rows, rows), rows)
    return pltpu.make_async_copy(w_ref.at[at], dst_ref.at[t], sem_ref.at[t])


def apply_mask(dst_ref, w_ref, m_ref, i, blk):
    for a in range(2):
        for j in range(w_ref.shape[1] // blk):
            keep = m_ref[2 * i + a, j].astype(F32).astype(BF16)
            ra, cj = slice(a * blk, (a + 1) * blk), slice(j * blk, (j + 1) * blk)
            dst_ref[ra, cj] = w_ref[ra, cj] * keep


def hidden_part(where, first, second, w, mask, swap):
    h, d = w.shape
    blk = h // mask.shape[0]
    m = first.shape[0]
    tile = 2 * blk

    def body(at_ref, m_ref, w_ref, a_ref, b_ref, keep_ref, send_ref, rows_ref, eff_ref, all_ref, sem_ref):
        j = pl.program_id(0)

        @pl.when(j == 0)
        def _():
            for t in range(h // tile):
                tile_copy(w_ref, all_ref, sem_ref, t).start()
            stack_rows(rows_ref, (a_ref, b_ref))

        tile_copy(w_ref, all_ref, sem_ref, j).wait()
        apply_mask(eff_ref, all_ref.at[j], m_ref, j, blk)
        out = lax.dot_general(rows_ref[...], eff_ref[...], NT, preferred_element_type=F32)
        one, two = out[:m], out[m:]
        if swap:
            here = at_ref[where.shape[0] - 1] == 0
            one, two = jnp.where(here, one, two), jnp.where(here, two, one)
        keep_ref[...] = one
        send_ref[...] = two.astype(BF16)

    out_spec = pl.BlockSpec((m, tile), lambda j: (0, j))
    return pl.pallas_call(
        body,
        grid=(h // tile,),
        in_specs=[
            smem_spec(),
            smem_spec(),
            pl.BlockSpec(memory_space=pl.ANY),
            whole_spec(first),
            whole_spec(second),
        ],
        out_specs=[out_spec, out_spec],
        out_shape=[jax.ShapeDtypeStruct((m, h), F32), jax.ShapeDtypeStruct((m, h), BF16)],
        scratch_shapes=[
            pltpu.VMEM((2 * m, d), BF16),
            pltpu.VMEM((tile, d), BF16),
            pltpu.VMEM((h // tile, tile, d), BF16),
            pltpu.SemaphoreType.DMA((h // tile,)),
        ],
        compiler_params=params(16),
        cost_estimate=cost(4 * m * d * h, 2 * d * (m + h) + 6 * m * h),
        name="hidden_part",
    )(where, mask, in_hbm(w), first, second)


def activation(saved, where):
    m, h = saved[0][0].shape
    n = len(saved)
    wide = 256 if h % 256 == 0 else 128

    def body(at_ref, *refs):
        o_ref, buf_ref, sem_ref = refs[2 * n :]
        k = pl.program_id(0)

        def copy(src, i, p):
            return pltpu.make_async_copy(refs[2 * src + p], buf_ref.at[i, p], sem_ref.at[i, p])

        @pl.when(k == 0)
        def _():
            for i in range(n):
                for p in range(2):
                    copy(i, i, p).start()

        for p in range(2):
            copy(0, k, p).wait()
        for c in range(h // wide):
            at = slice(c * wide, (c + 1) * wide)
            g = buf_ref[k, 0, :, at].astype(F32)
            u = buf_ref[k, 1, :, at].astype(F32)
            act = g * (1.0 / (1.0 + jnp.exp(-g))) * u
            o_ref[at, :] = act.astype(BF16).T

    return pl.pallas_call(
        body,
        grid=(n,),
        in_specs=[smem_spec()] + [pl.BlockSpec(memory_space=pl.ANY)] * (2 * n),
        out_specs=pl.BlockSpec((h, m), lambda k: (0, k)),
        out_shape=jax.ShapeDtypeStruct((h, n * m), BF16),
        scratch_shapes=[pltpu.VMEM((n, 2, m, h), BF16), pltpu.SemaphoreType.DMA((n, 2))],
        compiler_params=params(16),
        cost_estimate=cost(10 * h * n * m, 6 * h * n * m),
        name="activation",
    )(where, *[in_hbm(x) for x in saved[0]], *[x for pair in saved[1:] for x in pair])


def swiglu_grads(sums, saved, where, n, q):
    m, h = sums[0].shape
    cuts = 2 if (h // 2) % 128 == 0 else 1
    wide = h // cuts
    ns, nt = len(saved), len(sums)

    def body(i_ref, *refs):
        s_refs, t_refs = refs[: 2 * ns], refs[2 * ns : 2 * ns + nt]
        o_ref, s_buf = refs[2 * ns + nt], refs[2 * ns + nt + 1]
        t_bufs = refs[2 * ns + nt + 2 : 2 * ns + 2 * nt + 2]
        o_buf, s_sem, t_sem, o_sem = refs[2 * ns + 2 * nt + 2 :]
        src = i_ref[n] // q
        rows = pl.ds(pl.multiple_of(i_ref[n] % q * m, m), m)

        def saved_copy(c, k, p):
            cols = slice(c * wide, (c + 1) * wide)
            return pltpu.make_async_copy(
                s_refs[2 * k + p].at[rows, cols], s_buf.at[c, p], s_sem.at[c, p]
            )

        def term_copy(c, t):
            cols = slice(c * wide, (c + 1) * wide)
            return pltpu.make_async_copy(t_refs[t].at[:, cols], t_bufs[t].at[c], t_sem.at[c, t])

        def out_copy(c):
            cols = slice(c * wide, (c + 1) * wide)
            return pltpu.make_async_copy(o_buf.at[c], o_ref.at[:, :, cols], o_sem.at[c])

        for c in range(cuts):
            for k in range(ns):

                @pl.when(src == k)
                def _():
                    for p in range(2):
                        saved_copy(c, k, p).start()

            for t in range(nt):
                term_copy(c, t).start()
        for c in range(cuts):
            for p in range(2):
                saved_copy(c, 0, p).wait()
            for t in range(nt):
                term_copy(c, t).wait()
            hg = t_bufs[0][c].astype(F32)
            for t in range(1, nt):
                hg = hg + t_bufs[t][c].astype(F32)
            g = s_buf[c, 0].astype(F32)
            u = s_buf[c, 1].astype(F32)
            sig = 1.0 / (1.0 + jnp.exp(-g))
            hs = hg * sig
            o_buf[c, 0] = (hs * u * (1.0 + g * (1.0 - sig))).astype(BF16)
            o_buf[c, 1] = (hs * g).astype(BF16)
            out_copy(c).start()
        for c in range(cuts):
            out_copy(c).wait()

    anywhere = pl.BlockSpec(memory_space=pl.ANY)
    return pl.pallas_call(
        body,
        in_specs=[smem_spec()] + [anywhere] * (2 * ns + nt),
        out_specs=anywhere,
        out_shape=jax.ShapeDtypeStruct((2, m, h), BF16),
        scratch_shapes=[pltpu.VMEM((cuts, 2, m, wide), BF16)]
        + [pltpu.VMEM((cuts, m, wide), x.dtype) for x in sums]
        + [
            pltpu.VMEM((cuts, 2, m, wide), BF16),
            pltpu.SemaphoreType.DMA((cuts, 2)),
            pltpu.SemaphoreType.DMA((cuts, nt)),
            pltpu.SemaphoreType.DMA((cuts,)),
        ],
        compiler_params=params(8),
        cost_estimate=cost(20 * h * m, 14 * h * m),
        name="swiglu_grads",
    )(where, *[in_hbm(x) for pair in saved for x in pair], *sums)


def turned_weight(w, mask, where):
    d, h = w.shape
    nr, nc = mask.shape
    blk = d // nr
    tile = 2 * blk

    def body(at_ref, m_ref, w_ref, o_ref):
        i = pl.program_id(0)
        for j in range(nc):
            cols = slice(j * blk, (j + 1) * blk)
            halves = []
            for a in range(2):
                keep = m_ref[2 * i + a, j].astype(F32).astype(BF16)
                halves.append(w_ref[a * blk : (a + 1) * blk, cols] * keep)
            o_ref[0, cols, :] = jnp.concatenate(halves, 0).T

    return pl.pallas_call(
        body,
        grid=(d // tile,),
        in_specs=[smem_spec(), smem_spec(), pl.BlockSpec((tile, h), lambda i: (i, 0))],
        out_specs=pl.BlockSpec((1, h, tile), lambda i: (i, 0, 0)),
        out_shape=pltpu.HBM((d // tile, h, tile), BF16),
        compiler_params=params(8),
        cost_estimate=cost(d * h, 4 * d * h),
        name="turned_weight",
    )(where, mask, in_hbm(w))


def input_part(grads, gate_t, up_t, where):
    _, m, h = grads[0].shape
    n = len(grads)
    tiles, _, tile = gate_t.shape
    d = tiles * tile

    def body(at_ref, wg_ref, wu_ref, *refs):
        o_ref, g_ref, u_ref, wg_all, wu_all, g_sem, u_sem = refs[n:]
        i = pl.program_id(0)

        def copies(t):
            return (
                pltpu.make_async_copy(wg_ref.at[t], wg_all.at[t], g_sem.at[t]),
                pltpu.make_async_copy(wu_ref.at[t], wu_all.at[t], u_sem.at[t]),
            )

        @pl.when(i == 0)
        def _():
            for t in range(tiles):
                for copy in copies(t):
                    copy.start()
            stack_rows(g_ref, [r.at[0] for r in refs[:n]])
            stack_rows(u_ref, [r.at[1] for r in refs[:n]])

        for copy in copies(i):
            copy.wait()
        out = lax.dot_general(g_ref[...], wg_all[i], NN, preferred_element_type=F32)
        out = out + lax.dot_general(u_ref[...], wu_all[i], NN, preferred_element_type=F32)
        for k in range(n):
            o_ref[k] = out[k * m : (k + 1) * m]

    anywhere = pl.BlockSpec(memory_space=pl.ANY)
    return pl.pallas_call(
        body,
        grid=(tiles,),
        in_specs=[smem_spec(), anywhere, anywhere] + [whole_spec(x) for x in grads],
        out_specs=pl.BlockSpec((n, m, tile), lambda j: (0, 0, j)),
        out_shape=jax.ShapeDtypeStruct((n, m, d), F32),
        scratch_shapes=[pltpu.VMEM((n * m, h), BF16)] * 2
        + [pltpu.VMEM((tiles, h, tile), BF16)] * 2
        + [pltpu.SemaphoreType.DMA((tiles,))] * 2,
        compiler_params=params(28),
        cost_estimate=cost(4 * n * m * d * h, 4 * n * m * h + 4 * d * h + 4 * n * m * d),
        name="input_part",
    )(where, in_hbm(gate_t), in_hbm(up_t), *grads)


def weight_grad(lhs, rhs, mask, where, pick=None, places=None):
    lhs = lhs if isinstance(lhs, list) else [lhs]
    rows = lhs[0].shape[0]
    k = sum(x.shape[1] for x in lhs)
    cols = rhs[0].shape[-1]
    nr, nc = mask.shape
    blk = rows // nr
    per = 4 if nr % 4 == 0 else 2
    tile = per * blk
    wide = 2 * blk
    nl, n = len(lhs), len(rhs)

    def body(m_ref, p_ref, *refs):
        lefts, rights = refs[:nl], refs[nl : nl + n]
        o_ref, r_ref, l_ref = refs[nl + n :]
        i = pl.program_id(0)

        @pl.when(i == 0)
        def _():
            if places is None:
                stack_rows(r_ref, [r if pick is None else r.at[0] for r in rights])
            else:
                for t, r in enumerate(rights):
                    m = r.shape[0]
                    r_ref[pl.ds(pl.multiple_of(p_ref[places + t] * m, m), m)] = r[...]

        if nl > 1:
            at = 0
            for r in lefts:
                l_ref[:, at : at + r.shape[1]] = r[...]
                at += r.shape[1]
        left = l_ref if nl > 1 else lefts[0]
        for c in range(cols // wide):
            out = lax.dot_general(
                left[...], r_ref[:, c * wide : (c + 1) * wide], NN, preferred_element_type=F32
            )
            for a in range(per):
                for s in range(2):
                    keep = m_ref[i * per + a, 2 * c + s].astype(F32)
                    ra, cs = slice(a * blk, (a + 1) * blk), slice(s * blk, (s + 1) * blk)
                    at = slice((2 * c + s) * blk, (2 * c + s + 1) * blk)
                    o_ref[ra, at] = (out[ra, cs] * keep).astype(BF16)

    specs = [pl.BlockSpec((tile, x.shape[1]), lambda i: (i, 0)) for x in lhs]
    for r in rhs:
        if pick is None:
            specs.append(whole_spec(r))
        else:
            specs.append(
                pl.BlockSpec(
                    (1,) + r.shape[1:], lambda i: (pick, 0, 0), pipeline_mode=pl.Buffered(1)
                )
            )
    return pl.pallas_call(
        body,
        grid=(rows // tile,),
        in_specs=[smem_spec(), smem_spec()] + specs,
        out_specs=pl.BlockSpec((tile, cols), lambda i: (i, 0)),
        out_shape=jax.ShapeDtypeStruct((rows, cols), BF16),
        scratch_shapes=[
            pltpu.VMEM((k, cols), BF16),
            pltpu.VMEM((tile, k) if nl > 1 else (16, 128), BF16),
        ],
        compiler_params=params(20),
        cost_estimate=cost(2 * rows * cols * k, 2 * (rows * k + cols * k + rows * cols)),
        name="weight_grad",
    )(mask, where, *lhs, *rhs)


def join(*xs):
    return lax.optimization_barrier(xs)


def ring_order(n):
    a = 4 if n % 4 == 0 and n > 4 else 2
    b = n // a
    walk = [(0, j) for j in range(b)]
    for i in range(1, a):
        js = range(b - 1, 0, -1) if i % 2 else range(1, b)
        walk += [(i, j) for j in js]
    walk += [(i, 0) for i in range(a - 1, 0, -1)]
    return [i * b + j for i, j in walk]


def per_device(
    n_row, n_col, inputs, grad_out, gate_pre, up_pre, w_gate, w_up, w_down, mask_gate, mask_up, mask_down
):
    order = ring_order(n_col)
    half = n_col // 2
    ny = n_row // 2
    tpc = inputs.shape[0]
    q = gate_pre.shape[0] // tpc
    row = lax.axis_index("row")
    core = row % 2
    first = core == 0

    def ring_perm(step):
        pairs = []
        for r in range(n_row):
            s = step if r % 2 == 0 else -step
            for p in range(n_col):
                pairs.append((r * n_col + order[p], r * n_col + order[(p + s) % n_col]))
        return pairs

    back, ahead = ring_perm(-1), ring_perm(1)

    def from_ahead(x):
        return lax.ppermute(x, ("row", "col"), back)

    def from_behind(x):
        return lax.ppermute(x, ("row", "col"), ahead)

    def swap_core(x):
        return lax.ppermute(x, "row", [(r, r ^ 1) for r in range(n_row)])

    def shift_y(x, s):
        return lax.ppermute(
            x, "row", [(r, (r // 2 + s) % ny * 2 + r % 2) for r in range(n_row)]
        )

    last = half - 1
    dists = list(range(1, half)) + [0] + [s * d for d in range(1, half) for s in (1, -1)] + [0, half]
    at = lax.iota(jnp.int32, len(dists) + 1)
    dist = jnp.zeros_like(at)
    for i, d in enumerate(dists):
        if d:
            dist = jnp.where(at == i, d, dist)
    dist = jnp.where(at == last, core * half, dist)
    col = lax.axis_index("col")
    pos = sum(jnp.where(col == c, p, 0) for p, c in enumerate(order))
    near = (pos + (1 - 2 * core) * dist + 2 * n_col) % n_col
    block = sum(jnp.where(near == p, c, 0) for p, c in enumerate(order))
    owner = block // q
    s = (row // 2 - owner // 2 + ny) % ny
    e = (owner % 2 + core) % 2
    where = jnp.where(at == len(dists), core, (s * 2 + e) * q + block % q).astype(jnp.int32)

    def spread_y(x):
        return [shift_y(x, s) for s in range(1, ny)]

    go_rows, terms = [], []
    others, own, got, parts = [None] * half, [None] * half, [None] * half, [None] * half

    def hidden(n, x, y, after):
        kept, sent = hidden_part(after, x, y, w_down, mask_down, n == last)
        go_rows.extend([x, y])
        terms.append([kept, swap_core(sent)])

    def chip_sum(n):
        chip = (terms[n][0] + terms[n][1].astype(F32)).astype(BF16)
        return chip if n == last else jnp.pad(chip, ((0, 0), (0, 128)))

    def grads(n, after):
        sums = terms[n] + others[n]
        if n == half - 2:
            sums = [in_hbm(x) for x in sums]
        own[n] = swiglu_grads(sums, saved, after, n, q)

    def following(x):
        return join(where, x)[0]

    a, b = from_ahead(grad_out), from_behind(grad_out)
    gate_y, up_y, in_t = spread_y(gate_pre), spread_y(up_pre), inputs.T
    by_core = []
    gate_t = turned_weight(w_gate, mask_gate, where)
    a, b, where, in_t, gate_t, *by_core = join(a, b, where, in_t, gate_t, *by_core)

    up_t, y_core = None, []
    for k in range(2, half + 1):
        na = from_ahead(a)
        nb = from_behind(b) if k < half else b
        after = where
        if k > 2:
            chip = chip_sum(k - 3)
            after = following(chip)
        hidden(k - 2, a, b, after)
        over, more = [], []
        if k > 2:
            over = others[k - 3] = spread_y(chip)
        if k == 2:
            up_t = turned_weight(w_up, mask_up, following(terms[0][0]))
            more = gate_y + up_y + [up_t]
        elif k == 3:
            by_core = [swap_core(gate_pre)]
            more = by_core
        elif k == 4:
            by_core = by_core + [swap_core(up_pre)]
            y_core = [swap_core(x) for x in gate_y + up_y]
            saved = [(gate_pre, up_pre), tuple(by_core)]
            for s in range(ny - 1):
                saved += [(gate_y[s], up_y[s]), (y_core[s], y_core[ny - 1 + s])]
            act_t = activation(saved, following(terms[2][0]))
            more = [act_t]
        out = join(*over, na, nb, where, *more, *terms[k - 2])
        others[k - 3] = list(out[: len(over)]) if over else others[k - 3]
        a, b, where = out[len(over) : len(over) + 3]
        terms[k - 2], more = list(out[-2:]), list(out[len(over) + 3 : -2])
        if k == 2:
            gate_y, up_y, up_t = more[: ny - 1], more[ny - 1 : -1], more[-1]
        elif k == 3:
            by_core = more
        elif k == 4:
            act_t = more[0]
    far, in_t = join(a, in_t)
    ia, ib = from_ahead(in_t), from_behind(in_t)
    chip = chip_sum(half - 2)
    others[half - 2] = spread_y(chip)
    hidden(last, grad_out, far, following(chip))
    after = following(terms[last][0])
    for n in range(half - 2):
        grads(n, after)
        after = following(own[n])
    ia, ib, where, own[half - 3], *rest = join(ia, ib, where, own[half - 3], *others[half - 2])
    others[half - 2] = rest
    in_pairs = [(ia, ib)]

    ia, ib = from_ahead(ia), from_behind(ib)
    chip = chip_sum(last)
    others[last], after = spread_y(chip), following(chip)
    for n in range(half - 2):
        got[n] = swap_core(own[n])
    grad_down = weight_grad(act_t, go_rows, mask_down, after, places=half)
    ia, ib, where, grad_down, *rest = join(
        ia, ib, where, grad_down, *others[last], *got[: half - 2]
    )
    others[last], got[: half - 2] = rest[: ny - 1], rest[ny - 1 :]
    in_pairs.append((ia, ib))

    for _ in range(2, half - 1):
        ia, ib = from_ahead(ia), from_behind(ib)
        in_pairs.append((ia, ib))
    grads(last, where)
    got[last] = swap_core(own[last])
    grads(half - 2, following(own[last]))
    got[half - 2] = swap_core(own[half - 2])

    def part(ns, after):
        rows = [x for n in ns for x in (own[n], got[n])]
        return input_part(rows, gate_t, up_t, after)

    both = part([last], following(own[half - 2]))
    to_self = jnp.where(first, both[0], both[1])
    to_far = jnp.where(first, both[1], both[0]).astype(BF16)
    to_far, where, *early = join(to_far, where, *in_pairs[-1], *got[: half - 2])
    in_pairs[-1] = tuple(early[:2])
    got[: half - 2] = early[2:]
    ia = in_pairs[-1][0]

    run_a, run_b, in_far = from_behind(to_far), None, from_ahead(ia)
    parts[half - 2] = part([half - 2], where)
    run_a, where, parts[half - 2] = join(run_a, where, parts[half - 2])

    def send_sums(d):
        add_a = parts[d - 1][0] + run_a.astype(F32)
        add_b = parts[d - 1][1] + run_b.astype(F32) if run_b is not None else parts[d - 1][1]
        return from_behind(add_a.astype(BF16)), from_ahead(add_b.astype(BF16))

    run_a, run_b = send_sums(half - 1)
    both = part(list(range(half - 2)), where)
    lefts = [x for pair in in_pairs for x in pair]
    lefts += [jnp.where(first, in_t, in_far), jnp.where(first, in_far, in_t)]
    rights = [x for n in range(half) for x in (own[n], got[n])]
    run_a, run_b, where, both, *lefts = join(run_a, run_b, where, both, *lefts)
    for n in range(half - 2):
        parts[n] = both[2 * n : 2 * n + 2]

    grad_gate = grad_up = None
    for d in range(half - 2, 0, -1):
        run_a, run_b = send_sums(d)
        if d == half - 2:
            grad_gate = weight_grad(lefts, rights, mask_gate, where, 0)
            run_a, run_b, where, grad_gate = join(run_a, run_b, where, grad_gate)
        elif d == half - 3:
            grad_up = weight_grad(lefts, rights, mask_up, where, 1)
    grad_inputs = (to_self + run_a.astype(F32) + run_b.astype(F32)).astype(BF16)
    return (grad_inputs, grad_gate, grad_up, grad_down)


def solution(mesh):
    placed = (
        P("col", "row"),
        P("col", "row"),
        P("row", "col"),
        P("row", "col"),
        P("row", "col"),
        P("row", "col"),
        P("col", "row"),
        P("row", "col"),
        P("row", "col"),
        P("col", "row"),
    )
    return jax.shard_map(
        functools.partial(per_device, mesh.shape["row"], mesh.shape["col"]),
        mesh=mesh,
        in_specs=placed,
        out_specs=(P("col", "row"), P("row", "col"), P("row", "col"), P("col", "row")),
        check_vma=False,
    )
```
